32 devices in a mesh: ctx: 16 (over z, x, core), mp: 2 (over y).
Axes of the slice: x: 2, y: 2, z: 4, core: 2. Of those that a mesh axis runs over, the one named last changes fastest.
Arguments:
- byte_qkv: bfloat16 [8192, 3, 4096], P('ctx', None, 'mp'), may hold values from -14 to 14
- kv_weight: bfloat16 [4096, 2, 4096], P(None, None, 'mp'), may hold values from -4 to 4
- patch_bounds: int32 [16, 161], replicated, may hold values from 0 to 8192, as said below
Outputs:
- mixed: bfloat16 [2560, 4096], P('ctx', 'mp')
The draws below stay inside these ranges and needn't reach their ends.
Inputs may be any that keep to these rules, and one draw needn't show every extreme that they name: `patch_bounds`: row c lists in increasing order the first bytes of the patches that begin in bytes c * 512 to (c + 1) * 512 - 1, then the end of its last patch, repeated to the end of the row. The patches cover all 8192 bytes, each is 1 to 16 bytes long, one is exactly 16 long, and some row lists exactly 160 patches.
All inputs are finite; a program needn't handle non-finite values.
Results may differ from the reference program's by a relative error of at most 0.002.
The reference program's roundings to bfloat16 on the way count: a program that leaves them out, or rounds other values in their place, can miss the bound.
Values may be sent and summed in bfloat16 or wider, within the bound.
No kernel may reach another device: no remote copies, remote signals or barrier semaphores. Data moves between devices by JAX's collectives and lax.ppermute only.
A program may use at most 192 MiB of HBM per device.

```python
import math
import jax
import jax.numpy as jnp
from jax import lax

D = 4096
HEADS = 32
WIN = 16
BYTE_DEV = 512
PCAP = 160
BYTES = 8192
N_CTX = 16


def draw_byte_qkv(key, part):
    base = jax.random.fold_in(key, 29)
    key_noise = jax.random.fold_in(base, 0)
    component = jnp.array([1.0, 1.0, 2.0], jnp.float32)[None, :, None]
    whole = jnp.clip(jax.random.normal(key_noise, (BYTES, 3, D), jnp.float32), -6.0, 6.0) * component
    return whole.astype(jnp.bfloat16)


def draw_kv_weight(key, part):
    base = jax.random.fold_in(key, 5)
    weight_scale = 2.0 / math.sqrt(D)
    whole = jnp.clip(jax.random.normal(base, (D, 2, D), jnp.float32), -6.0, 6.0) * weight_scale
    return whole.astype(jnp.bfloat16)


def draw_patch_bounds(key, part):
    base = jax.random.fold_in(key, 17)
    key_offset, key_counts, key_full, key_order = jax.random.split(base, 4)
    lattice_count = BYTE_DEV // WIN
    offset = jax.random.randint(key_offset, (), 1, WIN)
    device = jnp.arange(N_CTX, dtype=jnp.int32)
    extra_cap = PCAP - lattice_count - (device == 0).astype(jnp.int32)
    extra = jax.random.randint(key_counts, (N_CTX,), 0, extra_cap + 1)
    fullest = jax.random.randint(key_full, (), 0, N_CTX)
    extra = jnp.where(device == fullest, extra_cap, extra)
    position = jnp.arange(BYTE_DEV, dtype=jnp.int32)
    lattice = (position >= offset) & ((position - offset) % WIN == 0)
    reserved = (position < offset + WIN) | (position > offset + BYTE_DEV - WIN)
    free_spot = jnp.logical_not(lattice) & jnp.logical_not(reserved)
    priority = jax.random.permutation(key_order, N_CTX * BYTE_DEV).astype(jnp.int32).reshape(N_CTX, BYTE_DEV)
    ranked = jnp.where(free_spot[None, :], priority, N_CTX * BYTE_DEV)
    cutoff = jnp.take_along_axis(jnp.sort(ranked, axis=1), extra[:, None], axis=1)
    chosen = free_spot[None, :] & (ranked < cutoff)
    first_byte = (device[:, None] == 0) & (position[None, :] == 0)
    is_start = lattice[None, :] | chosen | first_byte
    sort_key = jnp.sort(jnp.where(is_start, position[None, :], 2 * BYTE_DEV), axis=1)[:, :PCAP + 1]
    row_end = jnp.where(device < N_CTX - 1, (device + 1) * BYTE_DEV + offset, N_CTX * BYTE_DEV)
    result = jnp.where(sort_key < BYTE_DEV, device[:, None] * BYTE_DEV + sort_key, row_end[:, None])
    return result.astype(jnp.int32)


def setup_inputs(seed: int = 0) -> dict:
    key_of = jax.random.split(jax.random.key(seed), 4)
    byte_qkv = draw_byte_qkv(jax.random.fold_in(key_of[3], 71), 0)
    kv_weight = draw_kv_weight(jax.random.fold_in(key_of[3], 71), 0)
    patch_bounds = draw_patch_bounds(jax.random.fold_in(key_of[3], 71), 0)
    return dict(byte_qkv=byte_qkv, kv_weight=kv_weight, patch_bounds=patch_bounds)


masked_score = -1e+30

def reference(byte_qkv, kv_weight, patch_bounds):
    slot_total = N_CTX * PCAP
    head_dim = D // HEADS
    score_scale = 1.0 / math.sqrt(head_dim)
    starts = patch_bounds[:, :PCAP].reshape(slot_total)
    lengths = patch_bounds[:, 1:].reshape(slot_total) - starts
    live_slot = lengths > 0
    offsets = jnp.arange(WIN, dtype=jnp.int32)
    byte_index = jnp.clip(starts[:, None] + offsets[None, :], 0, BYTES - 1).astype(jnp.int32)
    inside = offsets[None, :] < lengths[:, None]

    def cross_head(head_index):
        columns = lax.dynamic_slice_in_dim(byte_qkv, head_index * head_dim, head_dim, 2)
        window = columns[byte_index]
        queries = lax.optimization_barrier(jnp.max(jnp.where(inside[:, :, None], window[:, :, 0], -jnp.inf), axis=1))
        queries = jnp.where(live_slot[:, None], queries, 0).astype(jnp.bfloat16)
        scores = jnp.einsum('sd,swd->sw', queries.astype(jnp.float32), window[:, :, 1].astype(jnp.float32)) * score_scale
        scores = jnp.where(inside, scores, masked_score)
        scores = scores - lax.optimization_barrier(jnp.max(scores, axis=1, keepdims=True))
        exp_terms = jnp.exp(scores)
        weights = (exp_terms / lax.optimization_barrier(jnp.sum(exp_terms, axis=1, keepdims=True))).astype(jnp.bfloat16)
        pooled = jnp.einsum('sw,swd->sd', weights.astype(jnp.float32), window[:, :, 2].astype(jnp.float32))
        return jnp.where(live_slot[:, None], pooled, 0.0).astype(jnp.bfloat16)
    heads_out = lax.map(cross_head, jnp.arange(HEADS, dtype=jnp.int32))
    patch_state = heads_out.transpose(1, 0, 2).reshape(slot_total, D)
    key_part = jnp.dot(patch_state, kv_weight[:, 0, :], preferred_element_type=jnp.float32).astype(jnp.bfloat16)
    value_part = jnp.dot(patch_state, kv_weight[:, 1, :], preferred_element_type=jnp.float32).astype(jnp.bfloat16)
    slot_order = jnp.arange(slot_total, dtype=jnp.int32)
    visible = (slot_order[None, :] <= slot_order[:, None]) & live_slot[None, :]

    def global_head(head_index):
        query_cols = lax.dynamic_slice_in_dim(patch_state, head_index * head_dim, head_dim, 1)
        key_cols = lax.dynamic_slice_in_dim(key_part, head_index * head_dim, head_dim, 1)
        value_cols = lax.dynamic_slice_in_dim(value_part, head_index * head_dim, head_dim, 1)
        scores = jnp.dot(query_cols, key_cols.T, preferred_element_type=jnp.float32) * score_scale
        scores = jnp.where(visible, scores, masked_score)
        scores = scores - lax.optimization_barrier(jnp.max(scores, axis=1, keepdims=True))
        exp_terms = jnp.where(visible, jnp.exp(scores), 0.0)
        weights = exp_terms / lax.optimization_barrier(jnp.sum(exp_terms, axis=1, keepdims=True))
        result = jnp.dot(weights, value_cols.astype(jnp.float32), precision=lax.Precision.HIGHEST)
        return jnp.where(live_slot[:, None], result, 0.0)
    attended = lax.map(global_head, jnp.arange(HEADS, dtype=jnp.int32))
    attended = attended.transpose(1, 0, 2).reshape(slot_total, D)
    return (patch_state.astype(jnp.float32) + attended).astype(jnp.bfloat16)
```

```python
import functools
import math

import jax
import jax.numpy as jnp
from jax import lax
from jax.experimental import pallas as pl
from jax.experimental.pallas import tpu as pltpu
from jax.sharding import PartitionSpec as P

D = 4096
HEADS = 32
WIN = 16
HEAD = D // HEADS
SCALE = 1.0 / math.sqrt(HEAD)
MASKED = -1e30
VMEM_LIMIT = 56 * 1024 * 1024


def params():
    return pltpu.CompilerParams(vmem_limit_bytes=VMEM_LIMIT)


def dot_f32(left, right, right_dim=0):
    return lax.dot_general(
        left, right, (((1,), (right_dim,)), ((), ())), preferred_element_type=jnp.float32
    )


def patch_body(heads, place_ref, bounds_ref, main_ref, edge_ref, out_ref, pens, bias, pick, live):
    byte_rows = main_ref.shape[1]
    slots = out_ref.shape[0]
    rows = byte_rows + WIN
    entries = bounds_ref.shape[1]

    @pl.when(pl.program_id(0) == 0)
    def _():
        place = place_ref[0]
        local = (bounds_ref[pl.ds(place, 1), :] - place * byte_rows).astype(jnp.float32)
        entry = lax.broadcasted_iota(jnp.int32, (slots, entries), 1)
        slot = lax.broadcasted_iota(jnp.int32, (slots, entries), 0)
        first = jnp.sum(jnp.where(entry == slot, local, 0.0), axis=1, keepdims=True)
        after = jnp.sum(jnp.where(entry == slot + 1, local, 0.0), axis=1, keepdims=True)
        byte = lax.broadcasted_iota(jnp.int32, (slots, rows), 1).astype(jnp.float32)
        inside = (byte >= first) & (byte < after)
        bias[...] = jnp.where(inside, 0.0, MASKED)
        pick[...] = jnp.where(inside & (byte == first), 1.0, 0.0).astype(jnp.bfloat16)
        live[...] = jnp.where(after > first, 1.0, 0.0)
        at = lax.broadcasted_iota(jnp.int32, (rows, entries), 0).astype(jnp.float32)
        begins = jnp.max(jnp.where(at == local, 1.0, 0.0), axis=1, keepdims=True)
        pen = jnp.broadcast_to(jnp.where(begins > 0.0, -jnp.inf, 0.0), (rows, HEAD))
        pen = pltpu.roll(pen, rows - 1, 0)
        pens[0] = pen
        for level in range(1, 4):
            pen = pen + pltpu.roll(pen, rows - (1 << (level - 1)), 0)
            pens[level] = pen

    for head in range(heads):
        cols = slice(head * HEAD, (head + 1) * HEAD)
        top = jnp.concatenate([main_ref[0, :, cols], edge_ref[0, :, cols]], axis=0).astype(jnp.float32)
        for level in range(4):
            top = jnp.maximum(top, pltpu.roll(top, rows - (1 << level), 0) + pens[level])
        query = dot_f32(pick[...], top.astype(jnp.bfloat16)).astype(jnp.bfloat16)
        keys = jnp.concatenate([main_ref[1, :, cols], edge_ref[1, :, cols]], axis=0)
        values = jnp.concatenate([main_ref[2, :, cols], edge_ref[2, :, cols]], axis=0)
        scores = dot_f32(query, keys, 1) * SCALE + bias[...]
        terms = jnp.exp(scores - jnp.max(scores, axis=1, keepdims=True))
        total = jnp.sum(terms, axis=1, keepdims=True)
        weights = (terms * (live[...] / total)).astype(jnp.bfloat16)
        out_ref[:, cols] = dot_f32(weights, values).astype(jnp.bfloat16)


def patch_states(place, bounds, parts, edge, first_head, head_count, slots):
    byte_rows = parts.shape[1]
    rows = byte_rows + WIN
    group = 2 if head_count % 2 == 0 else 1
    skip = first_head // group
    width = group * HEAD
    return pl.pallas_call(
        functools.partial(patch_body, group),
        grid=(head_count // group,),
        in_specs=[
            pl.BlockSpec(memory_space=pltpu.SMEM),
            pl.BlockSpec(bounds.shape, lambda i: (0, 0)),
            pl.BlockSpec((3, byte_rows, width), lambda i: (0, 0, i + skip)),
            pl.BlockSpec((3, WIN, width), lambda i: (0, 0, i + skip)),
        ],
        out_specs=pl.BlockSpec((slots, width), lambda i: (0, i)),
        out_shape=jax.ShapeDtypeStruct((slots, head_count * HEAD), jnp.bfloat16),
        scratch_shapes=[
            pltpu.VMEM((4, rows, HEAD), jnp.float32),
            pltpu.VMEM((slots, rows), jnp.float32),
            pltpu.VMEM((slots, rows), jnp.bfloat16),
            pltpu.VMEM((slots, 1), jnp.float32),
        ],
        compiler_params=params(),
        name="patch_states",
    )(place, bounds, parts, edge)


def project_body(start_ref, states_ref, weight_ref, sums_ref):
    width = weight_ref.shape[2]

    @pl.when(pl.program_id(0) == 0)
    def _():
        sums_ref[...] = jnp.zeros_like(sums_ref)

    states = states_ref[...]
    sums_ref[:, :width] += dot_f32(states, weight_ref[:, 0, :])
    sums_ref[:, width:] += dot_f32(states, weight_ref[:, 1, :])


def project_more_body(start_ref, states_ref, weight_ref, before_ref, own_ref, out_ref, sums):
    width = weight_ref.shape[2]

    @pl.when(pl.program_id(0) == 0)
    def _():
        sums[...] = before_ref[...]

    states = states_ref[...]
    sums[:, :width] += dot_f32(states, weight_ref[:, 0, :])
    sums[:, width:] += dot_f32(states, weight_ref[:, 1, :])

    @pl.when(pl.program_id(0) == pl.num_programs(0) - 1)
    def _():
        for head in range(width // HEAD):
            cols = slice(head * HEAD, (head + 1) * HEAD)
            out_ref[head, :, :HEAD] = own_ref[:, cols]
            out_ref[head, :, HEAD : 2 * HEAD] = sums[:, cols].astype(jnp.bfloat16)
            out_ref[head, :, 2 * HEAD :] = sums[:, width + head * HEAD : width + (head + 1) * HEAD].astype(
                jnp.bfloat16
            )


def feature_chunk(count):
    return next(c for c in (512, 256, 128) if count % c == 0)


def project(start, states, weight):
    slots, count = states.shape
    width = weight.shape[2]
    chunk = feature_chunk(count)
    return pl.pallas_call(
        project_body,
        grid_spec=pltpu.PrefetchScalarGridSpec(
            num_scalar_prefetch=1,
            grid=(count // chunk,),
            in_specs=[
                pl.BlockSpec((slots, chunk), lambda i, start: (0, i)),
                pl.BlockSpec((chunk, 2, width), lambda i, start: (start[0] * (count // chunk) + i, 0, 0)),
            ],
            out_specs=pl.BlockSpec((slots, 2 * width), lambda i, start: (0, 0)),
        ),
        out_shape=jax.ShapeDtypeStruct((slots, 2 * width), jnp.float32),
        compiler_params=params(),
        name="project",
    )(start, states, weight)


def project_more(start, states, weight, before, own):
    slots, count = states.shape
    width = weight.shape[2]
    chunk = feature_chunk(count)
    heads = width // HEAD
    return pl.pallas_call(
        project_more_body,
        grid_spec=pltpu.PrefetchScalarGridSpec(
            num_scalar_prefetch=1,
            grid=(count // chunk,),
            in_specs=[
                pl.BlockSpec((slots, chunk), lambda i, start: (0, i)),
                pl.BlockSpec((chunk, 2, width), lambda i, start: (start[0] * (count // chunk) + i, 0, 0)),
                pl.BlockSpec((slots, 2 * width), lambda i, start: (0, 0)),
                pl.BlockSpec((slots, width), lambda i, start: (0, 0)),
            ],
            out_specs=pl.BlockSpec((heads, slots, 3 * HEAD), lambda i, start: (0, 0, 0)),
            scratch_shapes=[pltpu.VMEM((slots, 2 * width), jnp.float32)],
        ),
        out_shape=jax.ShapeDtypeStruct((heads, slots, 3 * HEAD), jnp.bfloat16),
        compiler_params=params(),
        name="project_more",
    )(start, states, weight, before, own)


def attend_body(block, bias_ref, qkv_ref, out_ref, values):
    slots = qkv_ref.shape[0]
    values[:, :HEAD] = qkv_ref[:, 2 * HEAD :]
    values[:, HEAD:] = jnp.ones((slots, HEAD), jnp.bfloat16)
    row = lax.broadcasted_iota(jnp.int32, (block, block), 0)
    col = lax.broadcasted_iota(jnp.int32, (block, block), 1)
    later = jnp.where(col <= row, 0.0, MASKED)
    for at in range(0, slots, block):
        seen = at + block
        query = qkv_ref[at:seen, :HEAD]
        scores = dot_f32(query, qkv_ref[:seen, HEAD : 2 * HEAD], 1) * SCALE + bias_ref[:, :seen]
        last = scores[:, at:] + later
        scores = last if at == 0 else jnp.concatenate([scores[:, :at], last], axis=1)
        terms = jnp.exp(scores - jnp.max(scores, axis=1, keepdims=True))
        high = terms.astype(jnp.bfloat16)
        low = (terms - high.astype(jnp.float32)).astype(jnp.bfloat16)
        summed = dot_f32(high, values[:seen]) + dot_f32(low, values[:seen])
        mixed = query.astype(jnp.float32) + summed[:, :HEAD] / summed[:, HEAD:]
        out_ref[at:seen] = mixed.astype(jnp.bfloat16)


def attend(bias, qkv):
    slots = qkv.shape[0]
    block = next(b for b in (256, 128) if slots % b == 0)
    return pl.pallas_call(
        functools.partial(attend_body, block),
        out_shape=jax.ShapeDtypeStruct((slots, HEAD), jnp.bfloat16),
        scratch_shapes=[pltpu.VMEM((slots, 2 * HEAD), jnp.bfloat16)],
        compiler_params=params(),
        name="attend",
    )(bias, qkv)


def attend_gathered(place, valid, queries, keys, values):
    slots, width = queries.shape
    heads = width // HEAD
    keys = lax.all_gather(keys, "ctx", axis=0, tiled=True)
    values = lax.all_gather(values, "ctx", axis=0, tiled=True)
    total = keys.shape[0]
    query_slot = place * slots + jnp.arange(slots, dtype=jnp.int32)
    visible = (jnp.arange(total, dtype=jnp.int32)[None, :] <= query_slot[:, None]) & valid[None, :]
    scores = jnp.einsum(
        "qhd,khd->hqk",
        queries.reshape(slots, heads, HEAD),
        keys.reshape(total, heads, HEAD),
        preferred_element_type=jnp.float32,
    )
    scores = jnp.where(visible[None], scores * SCALE, MASKED)
    terms = jnp.where(visible[None], jnp.exp(scores - jnp.max(scores, axis=2, keepdims=True)), 0.0)
    sums = jnp.sum(terms, axis=2)
    attended = jnp.einsum(
        "hqk,khd->hqd",
        terms,
        values.reshape(total, heads, HEAD).astype(jnp.float32),
        precision=lax.Precision.HIGHEST,
    )
    attended = attended / jnp.where(sums > 0, sums, 1.0)[:, :, None]
    attended = attended.transpose(1, 0, 2).reshape(slots, width)
    return (queries.astype(jnp.float32) + attended).astype(jnp.bfloat16)


def shards(byte_qkv, kv_weight, patch_bounds):
    width = byte_qkv.shape[2]
    heads = width // HEAD
    slots = patch_bounds.shape[1] - 1
    ctx_count, mp_count = lax.axis_size("ctx"), lax.axis_size("mp")
    place = lax.axis_index("ctx").astype(jnp.int32)
    half = lax.axis_index("mp").astype(jnp.int32)

    edge = lax.ppermute(byte_qkv[:WIN], "ctx", [(i + 1, i) for i in range(ctx_count - 1)])
    parts = byte_qkv.transpose(1, 0, 2)
    edge = edge.transpose(1, 0, 2)
    states = patch_states(place[None], patch_bounds, parts, edge, 0, heads, slots)

    if mp_count == 2:
        others = lax.ppermute(states, "mp", [(0, 1), (1, 0)])
        before = project(half[None], states, kv_weight)
        other_half = 1 - half
    else:
        others = lax.all_gather(states, "mp", axis=1, tiled=True)
        before = jnp.zeros((slots, 2 * width), jnp.float32)
        other_half = jnp.zeros_like(half)
    qkv = project_more(other_half[None], others, kv_weight, before, states)

    valid = patch_bounds[:, 1:] > patch_bounds[:, :-1]
    if ctx_count == heads:
        bias = jnp.where(valid, 0.0, MASKED).astype(jnp.float32).reshape(1, ctx_count * slots)
        mine = lax.all_to_all(qkv, "ctx", 0, 0, tiled=True).reshape(ctx_count * slots, 3 * HEAD)
        mixed = attend(bias, mine).reshape(ctx_count, slots, HEAD)
        mixed = lax.all_to_all(mixed, "ctx", 0, 0, tiled=True)
        mixed = mixed.transpose(1, 0, 2).reshape(slots, width)
    else:
        keys = qkv[:, :, HEAD : 2 * HEAD].transpose(1, 0, 2).reshape(slots, width)
        values = qkv[:, :, 2 * HEAD :].transpose(1, 0, 2).reshape(slots, width)
        mixed = attend_gathered(place, valid.reshape(-1), states, keys, values)
    live = lax.dynamic_index_in_dim(valid, place, 0, keepdims=False)
    return jnp.where(live[:, None], mixed, jnp.zeros_like(mixed))


def solution(mesh):
    return jax.shard_map(
        shards,
        mesh=mesh,
        in_specs=(P("ctx", None, "mp"), P(None, None, "mp"), P()),
        out_specs=P("ctx", "mp"),
        check_vma=False,
    )
```

```python
import functools
import math

import jax
import jax.numpy as jnp
from jax import lax
from jax.experimental import pallas as pl
from jax.experimental.pallas import tpu as pltpu
from jax.sharding import PartitionSpec as P

D = 4096
HEADS = 32
WIN = 16
HEAD = D // HEADS
SCALE = 1.0 / math.sqrt(HEAD)
MASKED = -1e30
VMEM_LIMIT = 56 * 1024 * 1024


def params():
    return pltpu.CompilerParams(vmem_limit_bytes=VMEM_LIMIT)


def dot_f32(left, right, right_dim=0):
    return lax.dot_general(
        left, right, (((1,), (right_dim,)), ((), ())), preferred_element_type=jnp.float32
    )


def patch_body(heads, place_ref, bounds_ref, main_ref, edge_ref, out_ref, pens, bias, pick, live):
    byte_rows = main_ref.shape[1]
    slots = out_ref.shape[1]
    rows = byte_rows + WIN
    entries = bounds_ref.shape[1]

    @pl.when(pl.program_id(0) == 0)
    def _():
        place = place_ref[0]
        local = (bounds_ref[pl.ds(place, 1), :] - place * byte_rows).astype(jnp.float32)
        entry = lax.broadcasted_iota(jnp.int32, (slots, entries), 1)
        slot = lax.broadcasted_iota(jnp.int32, (slots, entries), 0)
        first = jnp.sum(jnp.where(entry == slot, local, 0.0), axis=1, keepdims=True)
        after = jnp.sum(jnp.where(entry == slot + 1, local, 0.0), axis=1, keepdims=True)
        byte = lax.broadcasted_iota(jnp.int32, (slots, rows), 1).astype(jnp.float32)
        inside = (byte >= first) & (byte < after)
        bias[...] = jnp.where(inside, 0.0, MASKED)
        pick[...] = jnp.where(inside & (byte == first), 1.0, 0.0).astype(jnp.bfloat16)
        live[...] = jnp.where(after > first, 1.0, 0.0)
        at = lax.broadcasted_iota(jnp.int32, (rows, entries), 0).astype(jnp.float32)
        begins = jnp.max(jnp.where(at == local, 1.0, 0.0), axis=1, keepdims=True)
        pen = jnp.broadcast_to(jnp.where(begins > 0.0, -jnp.inf, 0.0), (rows, HEAD))
        pen = pltpu.roll(pen, rows - 1, 0)
        pens[0] = pen
        for level in range(1, 4):
            pen = pen + pltpu.roll(pen, rows - (1 << (level - 1)), 0)
            pens[level] = pen

    for head in range(heads):
        cols = slice(head * HEAD, (head + 1) * HEAD)
        top = jnp.concatenate([main_ref[0, :, cols], edge_ref[0, :, cols]], axis=0).astype(jnp.float32)
        for level in range(4):
            top = jnp.maximum(top, pltpu.roll(top, rows - (1 << level), 0) + pens[level])
        query = dot_f32(pick[...], top.astype(jnp.bfloat16)).astype(jnp.bfloat16)
        keys = jnp.concatenate([main_ref[1, :, cols], edge_ref[1, :, cols]], axis=0)
        values = jnp.concatenate([main_ref[2, :, cols], edge_ref[2, :, cols]], axis=0)
        scores = dot_f32(query, keys, 1) * SCALE + bias[...]
        terms = jnp.exp(scores - jnp.max(scores, axis=1, keepdims=True))
        total = jnp.sum(terms, axis=1, keepdims=True)
        weights = (terms * (live[...] / total)).astype(jnp.bfloat16)
        out_ref[head] = dot_f32(weights, values).astype(jnp.bfloat16)


def patch_states(place, bounds, parts, edge, first_head, head_count, slots):
    byte_rows = parts.shape[1]
    rows = byte_rows + WIN
    group = next(g for g in (4, 2, 1) if head_count % g == 0)
    skip = first_head // group
    width = group * HEAD
    return pl.pallas_call(
        functools.partial(patch_body, group),
        grid=(head_count // group,),
        in_specs=[
            pl.BlockSpec(memory_space=pltpu.SMEM),
            pl.BlockSpec(bounds.shape, lambda i: (0, 0)),
            pl.BlockSpec((3, byte_rows, width), lambda i: (0, 0, i + skip)),
            pl.BlockSpec((3, WIN, width), lambda i: (0, 0, i + skip)),
        ],
        out_specs=pl.BlockSpec((group, slots, HEAD), lambda i: (i, 0, 0)),
        out_shape=jax.ShapeDtypeStruct((head_count, slots, HEAD), jnp.bfloat16),
        scratch_shapes=[
            pltpu.VMEM((4, rows, HEAD), jnp.float32),
            pltpu.VMEM((slots, rows), jnp.float32),
            pltpu.VMEM((slots, rows), jnp.bfloat16),
            pltpu.VMEM((slots, 1), jnp.float32),
        ],
        compiler_params=params(),
        name="patch_states",
    )(place, bounds, parts, edge)


def column_block(width):
    return next(c for c in (512, 256, 128) if width % c == 0)


def spread_products(start_ref, states_ref, weight_ref, spread, blocks, arrived, emit):
    heads, slots = states_ref.shape[:2]
    count = heads * HEAD
    steps, _, _, block = blocks.shape
    rows = pl.ds(pl.multiple_of(start_ref[0] * count, count), count)
    copies = [
        pltpu.make_async_copy(
            weight_ref.at[rows, :, pl.ds(step * block, block)], blocks.at[step], arrived.at[step]
        )
        for step in range(steps)
    ]
    for copy in copies:
        copy.start()
    feature = lax.broadcasted_iota(jnp.int32, (HEAD, 2 * HEAD), 0)
    row = lax.broadcasted_iota(jnp.int32, (HEAD, 2 * HEAD), 1)
    for part in range(2):
        place = jnp.where(row == 2 * feature + part, 1.0, 0.0).astype(jnp.bfloat16)
        for head in range(heads):
            spread[part * slots : (part + 1) * slots, 2 * head * HEAD : 2 * (head + 1) * HEAD] = dot_f32(
                states_ref[head], place
            ).astype(jnp.bfloat16)
    for step in range(steps):
        copies[step].wait()
        emit(step * block, block, dot_f32(spread[...], blocks.at[step].reshape(2 * count, block)[...]))


def project_body(start_ref, states_ref, weight_ref, sums_ref, spread, blocks, arrived):
    def emit(at, block, product):
        sums_ref[:, at : at + block] = product

    spread_products(start_ref, states_ref, weight_ref, spread, blocks, arrived, emit)


def project_more_body(start_ref, states_ref, weight_ref, before_ref, out_ref, spread, blocks, arrived):
    slots = out_ref.shape[1]

    def emit(at, block, product):
        total = (before_ref[:, at : at + block] + product).astype(jnp.bfloat16)
        for col in range(0, block, HEAD):
            head = (at + col) // HEAD
            out_ref[head, :, :HEAD] = total[:slots, col : col + HEAD]
            out_ref[head, :, HEAD:] = total[slots:, col : col + HEAD]

    spread_products(start_ref, states_ref, weight_ref, spread, blocks, arrived, emit)


def project_call(body, name, out_shape, start, states, weight, *before):
    heads, slots, _ = states.shape
    width = weight.shape[2]
    block = column_block(width)
    count = heads * HEAD
    in_vmem = pl.BlockSpec(memory_space=pltpu.VMEM)
    return pl.pallas_call(
        body,
        in_specs=[pl.BlockSpec(memory_space=pltpu.SMEM), in_vmem, pl.BlockSpec(memory_space=pl.ANY)]
        + [in_vmem] * len(before),
        out_specs=in_vmem,
        out_shape=out_shape,
        scratch_shapes=[
            pltpu.VMEM((2 * slots, 2 * count), jnp.bfloat16),
            pltpu.VMEM((width // block, count, 2, block), jnp.bfloat16),
            pltpu.SemaphoreType.DMA((width // block,)),
        ],
        compiler_params=params(),
        cost_estimate=pl.CostEstimate(
            flops=8 * slots * count * width, bytes_accessed=4 * count * width, transcendentals=0
        ),
        name=name,
    )(start, states, weight, *before)


def project(start, states, weight):
    shape = jax.ShapeDtypeStruct((2 * states.shape[1], weight.shape[2]), jnp.float32)
    return project_call(project_body, "project", shape, start, states, weight)


def project_more(start, states, weight, before):
    shape = jax.ShapeDtypeStruct((weight.shape[2] // HEAD, states.shape[1], 2 * HEAD), jnp.bfloat16)
    return project_call(project_more_body, "project_more", shape, start, states, weight, before)


def attend_body(block, bias_ref, query_ref, kv_ref, out_ref, values):
    slots = kv_ref.shape[0]
    values[:, :HEAD] = kv_ref[:, HEAD:]
    values[:, HEAD:] = jnp.ones((slots, HEAD), jnp.bfloat16)
    row = lax.broadcasted_iota(jnp.int32, (block, block), 0)
    col = lax.broadcasted_iota(jnp.int32, (block, block), 1)
    later = jnp.where(col <= row, 0.0, MASKED)
    for at in range(0, slots, block):
        seen = at + block
        query = query_ref[at:seen]
        scores = dot_f32(query, kv_ref[:seen, :HEAD], 1) * SCALE + bias_ref[:, :seen]
        last = scores[:, at:] + later
        scores = last if at == 0 else jnp.concatenate([scores[:, :at], last], axis=1)
        terms = jnp.exp(scores - jnp.max(scores, axis=1, keepdims=True))
        high = terms.astype(jnp.bfloat16)
        low = (terms - high.astype(jnp.float32)).astype(jnp.bfloat16)
        summed = dot_f32(high, values[:seen]) + dot_f32(low, values[:seen])
        mixed = query.astype(jnp.float32) + summed[:, :HEAD] / summed[:, HEAD:]
        out_ref[at:seen] = mixed.astype(jnp.bfloat16)


def attend(bias, query, kv):
    slots = kv.shape[0]
    block = next(b for b in (256, 128) if slots % b == 0)
    return pl.pallas_call(
        functools.partial(attend_body, block),
        out_shape=jax.ShapeDtypeStruct((slots, HEAD), jnp.bfloat16),
        scratch_shapes=[pltpu.VMEM((slots, 2 * HEAD), jnp.bfloat16)],
        compiler_params=params(),
        name="attend",
    )(bias, query, kv)


def attend_gathered(place, valid, queries, keys, values):
    slots, width = queries.shape
    heads = width // HEAD
    keys = lax.all_gather(keys, "ctx", axis=0, tiled=True)
    values = lax.all_gather(values, "ctx", axis=0, tiled=True)
    total = keys.shape[0]
    query_slot = place * slots + jnp.arange(slots, dtype=jnp.int32)
    visible = (jnp.arange(total, dtype=jnp.int32)[None, :] <= query_slot[:, None]) & valid[None, :]
    scores = jnp.einsum(
        "qhd,khd->hqk",
        queries.reshape(slots, heads, HEAD),
        keys.reshape(total, heads, HEAD),
        preferred_element_type=jnp.float32,
    )
    scores = jnp.where(visible[None], scores * SCALE, MASKED)
    terms = jnp.where(visible[None], jnp.exp(scores - jnp.max(scores, axis=2, keepdims=True)), 0.0)
    sums = jnp.sum(terms, axis=2)
    attended = jnp.einsum(
        "hqk,khd->hqd",
        terms,
        values.reshape(total, heads, HEAD).astype(jnp.float32),
        precision=lax.Precision.HIGHEST,
    )
    attended = attended / jnp.where(sums > 0, sums, 1.0)[:, :, None]
    attended = attended.transpose(1, 0, 2).reshape(slots, width)
    return (queries.astype(jnp.float32) + attended).astype(jnp.bfloat16)


def shards(byte_qkv, kv_weight, patch_bounds):
    width = byte_qkv.shape[2]
    heads = width // HEAD
    slots = patch_bounds.shape[1] - 1
    ctx_count, mp_count = lax.axis_size("ctx"), lax.axis_size("mp")
    place = lax.axis_index("ctx").astype(jnp.int32)
    half = lax.axis_index("mp").astype(jnp.int32)

    edge = lax.ppermute(byte_qkv[:WIN], "ctx", [(i + 1, i) for i in range(ctx_count - 1)])
    parts = byte_qkv.transpose(1, 0, 2)
    edge = edge.transpose(1, 0, 2)
    states = patch_states(place[None], patch_bounds, parts, edge, 0, heads, slots)

    paired = ctx_count == heads
    if mp_count == 2:
        others = lax.ppermute(states, "mp", [(0, 1), (1, 0)])
        before = project(half[None], states, kv_weight)
        other_half = 1 - half
    else:
        others = lax.all_gather(states, "mp", axis=0, tiled=True)
        before = jnp.zeros((2 * slots, width), jnp.float32)
        other_half = jnp.zeros_like(half)
    if paired:
        query = lax.all_to_all(states, "ctx", 0, 0, tiled=True).reshape(ctx_count * slots, HEAD)
    kv = project_more(other_half[None], others, kv_weight, before)

    valid = patch_bounds[:, 1:] > patch_bounds[:, :-1]
    if paired:
        bias = jnp.where(valid, 0.0, MASKED).astype(jnp.float32).reshape(1, ctx_count * slots)
        kv = lax.all_to_all(kv, "ctx", 0, 0, tiled=True).reshape(ctx_count * slots, 2 * HEAD)
        mixed = attend(bias, query, kv).reshape(ctx_count, slots, HEAD)
        mixed = lax.all_to_all(mixed, "ctx", 0, 0, tiled=True)
        mixed = mixed.transpose(1, 0, 2).reshape(slots, width)
    else:
        query, keys, values = (
            part.transpose(1, 0, 2).reshape(slots, width)
            for part in (states, kv[:, :, :HEAD], kv[:, :, HEAD:])
        )
        mixed = attend_gathered(place, valid.reshape(-1), query, keys, values)
    live = lax.dynamic_index_in_dim(valid, place, 0, keepdims=False)
    return jnp.where(live[:, None], mixed, jnp.zeros_like(mixed))


def solution(mesh):
    return jax.shard_map(
        shards,
        mesh=mesh,
        in_specs=(P("ctx", None, "mp"), P(None, None, "mp"), P()),
        out_specs=P("ctx", "mp"),
        check_vma=False,
    )
```

```python
import functools
import math

import jax
import jax.numpy as jnp
from jax import lax
from jax.experimental import pallas as pl
from jax.experimental.pallas import tpu as pltpu
from jax.sharding import PartitionSpec as P

D = 4096
HEADS = 32
WIN = 16
HEAD = D // HEADS
SCALE = 1.0 / math.sqrt(HEAD)
MASKED = -1e30


def params(mebibytes):
    return pltpu.CompilerParams(vmem_limit_bytes=mebibytes * 1024 * 1024)


def dot_f32(left, right, right_dim=0):
    return lax.dot_general(
        left, right, (((1,), (right_dim,)), ((), ())), preferred_element_type=jnp.float32
    )


def ahead(row, steps):
    return pltpu.roll(row, row.shape[1] - steps, 1)


def patch_body(heads, joins, place_ref, bounds_ref, main_ref, edge_ref, *refs):
    if joins:
        earlier_ref, out_ref, whole_ref, pens, cuts, inside, pick = refs
    else:
        out_ref, pens, cuts, inside, pick = refs
    byte_rows = main_ref.shape[1]
    slots = out_ref.shape[1]
    rows = byte_rows + WIN
    lanes = inside.shape[1]
    entries = bounds_ref.shape[1]

    @pl.when(pl.program_id(0) == 0)
    def _():
        place = place_ref[0]
        local = (bounds_ref[pl.ds(place, 1), :] - place * byte_rows).astype(jnp.float32)
        entry = lax.broadcasted_iota(jnp.int32, (slots, entries), 1)
        slot = lax.broadcasted_iota(jnp.int32, (slots, entries), 0)
        first = jnp.sum(jnp.where(entry == slot, local, 0.0), axis=1, keepdims=True)
        after = jnp.sum(jnp.where(entry == slot + 1, local, 0.0), axis=1, keepdims=True)
        byte = lax.broadcasted_iota(jnp.int32, (slots, lanes), 1).astype(jnp.float32)
        member = (byte >= first) & (byte < after)
        inside[...] = jnp.where(member, 1.0, 0.0)
        pick[...] = jnp.where(member & (byte == first), 1.0, 0.0)[:, :rows].astype(jnp.bfloat16)
        edges = jnp.where((byte == first) | (byte == after), 1.0, 0.0)
        cut = jnp.where(jnp.max(edges, axis=0, keepdims=True) > 0.0, -jnp.inf, 0.0)
        cut = ahead(jnp.broadcast_to(cut, (8, lanes)), 1)
        cuts[0] = cut
        at = lax.broadcasted_iota(jnp.int32, (rows, entries), 0).astype(jnp.float32)
        begins = jnp.max(jnp.where(at == local, 1.0, 0.0), axis=1, keepdims=True)
        pen = jnp.broadcast_to(jnp.where(begins > 0.0, -jnp.inf, 0.0), (rows, HEAD))
        pen = pltpu.roll(pen, rows - 1, 0)
        pens[0] = pen
        for level in range(1, 4):
            steps = 1 << (level - 1)
            cut = cut + ahead(cut, steps)
            cuts[level] = cut
            pen = pen + pltpu.roll(pen, rows - steps, 0)
            pens[level] = pen

    score_rows = []
    for head in range(heads):
        cols = slice(head * HEAD, (head + 1) * HEAD)
        top = jnp.concatenate([main_ref[0, :, cols], edge_ref[0, :, cols]], axis=0).astype(jnp.float32)
        for level in range(4):
            top = jnp.maximum(top, pltpu.roll(top, rows - (1 << level), 0) + pens[level])
        query = dot_f32(pick[...], top.astype(jnp.bfloat16)).astype(jnp.bfloat16)
        spare = jnp.zeros((lanes - rows, HEAD), jnp.bfloat16)
        keys = jnp.concatenate([main_ref[1, :, cols], edge_ref[1, :, cols], spare], axis=0)
        scores = dot_f32(query, keys, 1) * inside[...]
        score_rows.append(jnp.sum(scores, axis=0, keepdims=True))
    scores = jnp.concatenate(score_rows + [jnp.zeros((8 - heads, lanes), jnp.float32)] * (heads < 8), axis=0)
    fore = back = scores
    for level in range(4):
        steps = 1 << level
        cut = cuts[level]
        fore = jnp.maximum(fore, ahead(fore, steps) + cut)
        back = jnp.maximum(back, pltpu.roll(back + cut, steps, 1))
    terms = jnp.exp((scores - jnp.maximum(fore, back)) * SCALE)
    fore = back = terms
    for level in range(4):
        steps = 1 << level
        keep = jnp.where(cuts[level] < 0.0, 0.0, 1.0)
        fore = fore + ahead(fore, steps) * keep
        back = back + pltpu.roll(back * keep, steps, 1)
    weights = terms / (fore + back - terms)
    for head in range(heads):
        cols = slice(head * HEAD, (head + 1) * HEAD)
        spare = jnp.zeros((lanes - rows, HEAD), jnp.bfloat16)
        values = jnp.concatenate([main_ref[2, :, cols], edge_ref[2, :, cols], spare], axis=0)
        spread = (inside[...] * weights[head : head + 1]).astype(jnp.bfloat16)
        out_ref[head] = dot_f32(spread, values).astype(jnp.bfloat16)
    if joins:
        whole_ref[: heads] = earlier_ref[...]
        whole_ref[heads:] = out_ref[...]


def patch_states(place, bounds, parts, edge, slots, first_head, heads, earlier=None):
    byte_rows = parts.shape[1]
    rows = byte_rows + WIN
    lanes = -(-rows // 128) * 128
    width = heads * HEAD
    run = first_head // heads
    joins = earlier is not None
    states = jax.ShapeDtypeStruct((heads, slots, HEAD), jnp.bfloat16)
    states_spec = pl.BlockSpec((heads, slots, HEAD), lambda i: (0, 0, 0))
    whole = jax.ShapeDtypeStruct((2 * heads, slots, HEAD), jnp.bfloat16)
    whole_spec = pl.BlockSpec((2 * heads, slots, HEAD), lambda i: (0, 0, 0))
    return pl.pallas_call(
        functools.partial(patch_body, heads, joins),
        grid=(1,),
        in_specs=[
            pl.BlockSpec(memory_space=pltpu.SMEM),
            pl.BlockSpec(bounds.shape, lambda i: (0, 0)),
            pl.BlockSpec((3, byte_rows, width), lambda i: (0, 0, run)),
            pl.BlockSpec((3, WIN, width), lambda i: (0, 0, run)),
        ]
        + [states_spec] * joins,
        out_specs=[states_spec, whole_spec] if joins else states_spec,
        out_shape=[states, whole] if joins else states,
        scratch_shapes=[
            pltpu.VMEM((4, rows, HEAD), jnp.float32),
            pltpu.VMEM((4, 8, lanes), jnp.float32),
            pltpu.VMEM((slots, lanes), jnp.float32),
            pltpu.VMEM((slots, rows), jnp.bfloat16),
        ],
        compiler_params=params(20),
        name="patch_states",
    )(place, bounds, parts, edge, *([earlier] if joins else []))


def column_block(width):
    return next(c for c in (512, 256, 128) if width % c == 0)


def spread_states(states_refs, spread):
    slots = states_refs[0].shape[1]
    feature = lax.broadcasted_iota(jnp.int32, (HEAD, 2 * HEAD), 0)
    row = lax.broadcasted_iota(jnp.int32, (HEAD, 2 * HEAD), 1)
    for part in range(2):
        place = jnp.where(row == 2 * feature + part, 1.0, 0.0).astype(jnp.bfloat16)
        at = 0
        for states_ref in states_refs:
            for head in range(states_ref.shape[0]):
                spread[part * slots : (part + 1) * slots, at : at + 2 * HEAD] = dot_f32(
                    states_ref[head], place
                ).astype(jnp.bfloat16)
                at += 2 * HEAD


def project_body(half_ref, states_ref, weight_ref, sums_ref, held_ref, spread, blocks, arrived, held_arrived):
    count = states_ref.shape[0] * HEAD
    steps, _, _, block = blocks.shape

    def rows(half):
        return pl.ds(pl.multiple_of(half * count, count), count)

    half = half_ref[0]
    copies = [
        pltpu.make_async_copy(
            weight_ref.at[rows(half), :, pl.ds(step * block, block)], blocks.at[step], arrived.at[step]
        )
        for step in range(steps)
    ]
    hold = pltpu.make_async_copy(weight_ref.at[rows(1 - half)], held_ref, held_arrived)
    for copy in copies:
        copy.start()
    hold.start()
    spread_states([states_ref], spread)
    for step in range(steps):
        copies[step].wait()
        weights = blocks.at[step].reshape(2 * count, block)[...]
        sums_ref[:, step * block : (step + 1) * block] = dot_f32(spread[...], weights)
    hold.wait()


def project(half, states, weight):
    heads, slots, _ = states.shape
    width = weight.shape[2]
    block = column_block(width)
    count = heads * HEAD
    in_vmem = pl.BlockSpec(memory_space=pltpu.VMEM)
    return pl.pallas_call(
        project_body,
        in_specs=[pl.BlockSpec(memory_space=pltpu.SMEM), in_vmem, pl.BlockSpec(memory_space=pl.ANY)],
        out_specs=[in_vmem, pl.BlockSpec(memory_space=pl.ANY)],
        out_shape=[
            jax.ShapeDtypeStruct((2 * slots, width), jnp.float32),
            pltpu.VMEM((count, 2, width), weight.dtype),
        ],
        scratch_shapes=[
            pltpu.VMEM((2 * slots, 2 * count), jnp.bfloat16),
            pltpu.VMEM((width // block, count, 2, block), jnp.bfloat16),
            pltpu.SemaphoreType.DMA((width // block,)),
            pltpu.SemaphoreType.DMA,
        ],
        compiler_params=params(28),
        cost_estimate=pl.CostEstimate(
            flops=8 * slots * count * width, bytes_accessed=8 * count * width, transcendentals=0
        ),
        name="project",
    )(half, states, weight)


def project_more_body(parts, *refs):
    states_refs, (weight_ref, before_ref, out_ref, spread) = refs[:parts], refs[parts:]
    slots = out_ref.shape[1]
    count, _, width = weight_ref.shape
    block = column_block(width)
    spread_states(states_refs, spread)
    flat = weight_ref.reshape(2 * count, width)
    for at in range(0, width, block):
        product = dot_f32(spread[...], flat[:, at : at + block])
        total = (before_ref[:, at : at + block] + product).astype(jnp.bfloat16)
        for col in range(0, block, HEAD):
            head = (at + col) // HEAD
            out_ref[head, :, :HEAD] = total[:slots, col : col + HEAD]
            out_ref[head, :, HEAD:] = total[slots:, col : col + HEAD]


def project_more(states, weight, before):
    slots = states[0].shape[1]
    count, _, width = weight.shape
    in_vmem = pl.BlockSpec(memory_space=pltpu.VMEM)
    return pl.pallas_call(
        functools.partial(project_more_body, len(states)),
        in_specs=[in_vmem] * (len(states) + 2),
        out_specs=in_vmem,
        out_shape=jax.ShapeDtypeStruct((width // HEAD, slots, 2 * HEAD), jnp.bfloat16),
        scratch_shapes=[pltpu.VMEM((2 * slots, 2 * count), jnp.bfloat16)],
        compiler_params=params(24),
        cost_estimate=pl.CostEstimate(
            flops=8 * slots * count * width, bytes_accessed=4 * count * width, transcendentals=0
        ),
        name="project_more",
    )(*states, pltpu.with_memory_space_constraint(weight, pltpu.VMEM), before)


def attend_body(block, bias_ref, query_ref, kv_ref, out_ref, values):
    slots = kv_ref.shape[0]
    values[:, :HEAD] = kv_ref[:, HEAD:]
    values[:, HEAD:] = jnp.ones((slots, HEAD), jnp.bfloat16)
    row = lax.broadcasted_iota(jnp.int32, (block, block), 0)
    col = lax.broadcasted_iota(jnp.int32, (block, block), 1)
    later = jnp.where(col <= row, 0.0, MASKED)
    for at in range(0, slots, block):
        seen = at + block
        query = query_ref[at:seen]
        scores = dot_f32(query, kv_ref[:seen, :HEAD], 1) * SCALE + bias_ref[:, :seen]
        last = scores[:, at:] + later
        scores = last if at == 0 else jnp.concatenate([scores[:, :at], last], axis=1)
        terms = jnp.exp(scores - jnp.max(scores, axis=1, keepdims=True))
        high = terms.astype(jnp.bfloat16)
        low = (terms - high.astype(jnp.float32)).astype(jnp.bfloat16)
        summed = dot_f32(high, values[:seen]) + dot_f32(low, values[:seen])
        mixed = query.astype(jnp.float32) + summed[:, :HEAD] / summed[:, HEAD:]
        out_ref[at:seen] = mixed.astype(jnp.bfloat16)


def attend(bias, query, kv):
    slots = kv.shape[0]
    block = next(b for b in (256, 128) if slots % b == 0)
    return pl.pallas_call(
        functools.partial(attend_body, block),
        out_shape=jax.ShapeDtypeStruct((slots, HEAD), jnp.bfloat16),
        scratch_shapes=[pltpu.VMEM((slots, 2 * HEAD), jnp.bfloat16)],
        compiler_params=params(24),
        name="attend",
    )(bias, query, kv)


def attend_gathered(place, valid, queries, keys, values):
    slots, width = queries.shape
    heads = width // HEAD
    keys = lax.all_gather(keys, "ctx", axis=0, tiled=True)
    values = lax.all_gather(values, "ctx", axis=0, tiled=True)
    total = keys.shape[0]
    query_slot = place * slots + jnp.arange(slots, dtype=jnp.int32)
    visible = (jnp.arange(total, dtype=jnp.int32)[None, :] <= query_slot[:, None]) & valid[None, :]
    scores = jnp.einsum(
        "qhd,khd->hqk",
        queries.reshape(slots, heads, HEAD),
        keys.reshape(total, heads, HEAD),
        preferred_element_type=jnp.float32,
    )
    scores = jnp.where(visible[None], scores * SCALE, MASKED)
    terms = jnp.where(visible[None], jnp.exp(scores - jnp.max(scores, axis=2, keepdims=True)), 0.0)
    sums = jnp.sum(terms, axis=2)
    attended = jnp.einsum(
        "hqk,khd->hqd",
        terms,
        values.reshape(total, heads, HEAD).astype(jnp.float32),
        precision=lax.Precision.HIGHEST,
    )
    attended = attended / jnp.where(sums > 0, sums, 1.0)[:, :, None]
    attended = attended.transpose(1, 0, 2).reshape(slots, width)
    return (queries.astype(jnp.float32) + attended).astype(jnp.bfloat16)


def shards(byte_qkv, kv_weight, patch_bounds):
    width = byte_qkv.shape[2]
    heads = width // HEAD
    slots = patch_bounds.shape[1] - 1
    ctx_count, mp_count = lax.axis_size("ctx"), lax.axis_size("mp")
    place = lax.axis_index("ctx").astype(jnp.int32)
    half = lax.axis_index("mp").astype(jnp.int32)

    edge = lax.ppermute(byte_qkv[:WIN], "ctx", [(i + 1, i) for i in range(ctx_count - 1)])
    parts = byte_qkv.transpose(1, 0, 2)
    edge = edge.transpose(1, 0, 2)
    in_hbm = functools.partial(pltpu.with_memory_space_constraint, memory_space=pltpu.HBM)
    byte_phase = functools.partial(
        patch_states, place[None], in_hbm(patch_bounds), in_hbm(parts), edge, slots
    )
    run = max(heads // 2, 1)
    first = byte_phase(0, run)
    states = first
    if heads > run:
        second, states = byte_phase(run, run, first)

    paired = ctx_count == heads
    if mp_count == 2:
        others = [lax.ppermute(run_states, "mp", [(0, 1), (1, 0)]) for run_states in (first, second)]
        before, held = project(half[None], states, kv_weight)
    else:
        others = [lax.all_gather(states, "mp", axis=0, tiled=True)]
        before, held = jnp.zeros((2 * slots, width), jnp.float32), kv_weight
    if paired:
        sent, others[0] = lax.optimization_barrier((states, others[0]))
        query = lax.all_to_all(sent, "ctx", 0, 0, tiled=True).reshape(ctx_count * slots, HEAD)
    kv = project_more(others, held, before)

    valid = patch_bounds[:, 1:] > patch_bounds[:, :-1]
    if paired:
        bias = jnp.where(valid, 0.0, MASKED).astype(jnp.float32).reshape(1, ctx_count * slots)
        kv = lax.all_to_all(kv, "ctx", 0, 0, tiled=True).reshape(ctx_count * slots, 2 * HEAD)
        mixed = attend(bias, query, kv).reshape(ctx_count, slots, HEAD)
        mixed = lax.all_to_all(mixed, "ctx", 0, 0, tiled=True)
        mixed = mixed.transpose(1, 0, 2).reshape(slots, width)
    else:
        query, keys, values = (
            part.transpose(1, 0, 2).reshape(slots, width)
            for part in (states, kv[:, :, :HEAD], kv[:, :, HEAD:])
        )
        mixed = attend_gathered(place, valid.reshape(-1), query, keys, values)
    live = lax.dynamic_index_in_dim(valid, place, 0, keepdims=False)
    return jnp.where(live[:, None], mixed, jnp.zeros_like(mixed))


def solution(mesh):
    return jax.shard_map(
        shards,
        mesh=mesh,
        in_specs=(P("ctx", None, "mp"), P(None, None, "mp"), P()),
        out_specs=P("ctx", "mp"),
        check_vma=False,
    )
```

```python
import functools
import math

import jax
import jax.numpy as jnp
from jax import lax
from jax.experimental import pallas as pl
from jax.experimental.pallas import tpu as pltpu
from jax.sharding import PartitionSpec as P

D = 4096
HEADS = 32
WIN = 16
HEAD = D // HEADS
SCALE = 1.0 / math.sqrt(HEAD)
SCALE_2 = SCALE * math.log2(math.e)
MASKED = -1e30


def params(mebibytes):
    return pltpu.CompilerParams(vmem_limit_bytes=mebibytes * 1024 * 1024)


def dot_f32(left, right, right_dim=0):
    return lax.dot_general(
        left, right, (((1,), (right_dim,)), ((), ())), preferred_element_type=jnp.float32
    )


def ahead(row, steps):
    return pltpu.roll(row, row.shape[1] - steps, 1)


def patch_body(heads, joins, place_ref, bounds_ref, main_ref, edge_ref, *refs):
    if joins:
        earlier_ref, out_ref, whole_ref, *refs = refs
    else:
        out_ref, *refs = refs
    pens, cuts, inside, pick, tops = refs
    byte_rows = main_ref.shape[1]
    slots = out_ref.shape[1]
    rows = byte_rows + WIN
    lanes = inside.shape[1]
    entries = bounds_ref.shape[1]

    @pl.when(pl.program_id(0) == 0)
    def _():
        place = place_ref[0]
        local = (bounds_ref[pl.ds(place, 1), :] - place * byte_rows).astype(jnp.float32)
        entry = lax.broadcasted_iota(jnp.int32, (slots, entries), 1)
        slot = lax.broadcasted_iota(jnp.int32, (slots, entries), 0)
        first = jnp.sum(jnp.where(entry == slot, local, 0.0), axis=1, keepdims=True)
        after = jnp.sum(jnp.where(entry == slot + 1, local, 0.0), axis=1, keepdims=True)
        byte = lax.broadcasted_iota(jnp.int32, (slots, lanes), 1).astype(jnp.float32)
        member = (byte >= first) & (byte < after)
        inside[...] = jnp.where(member, 1.0, 0.0)
        pick[...] = jnp.where(member & (byte == first), 1.0, 0.0)[:, :rows].astype(jnp.bfloat16)
        edges = jnp.where((byte == first) | (byte == after), 1.0, 0.0)
        cut = jnp.where(jnp.max(edges, axis=0, keepdims=True) > 0.0, -jnp.inf, 0.0)
        cut = ahead(jnp.broadcast_to(cut, (8, lanes)), 1)
        cuts[0] = cut
        at = lax.broadcasted_iota(jnp.int32, (rows, entries), 0).astype(jnp.float32)
        begins = jnp.max(jnp.where(at == local, 1.0, 0.0), axis=1, keepdims=True)
        pen = jnp.broadcast_to(jnp.where(begins > 0.0, -jnp.inf, 0.0), (rows, HEAD))
        pen = pltpu.roll(pen, rows - 1, 0)
        pens[0] = pen
        for level in range(1, 4):
            steps = 1 << (level - 1)
            cut = cut + ahead(cut, steps)
            cuts[level] = cut
            pen = pen + pltpu.roll(pen, rows - steps, 0)
            pens[level] = pen

    for head in range(heads):
        cols = slice(head * HEAD, (head + 1) * HEAD)
        top = jnp.concatenate([main_ref[0, :, cols], edge_ref[0, :, cols]], axis=0).astype(jnp.float32)
        for level in range(4):
            top = jnp.maximum(top, pltpu.roll(top, rows - (1 << level), 0) + pens[level])
        tops[:, cols] = top.astype(jnp.bfloat16)
    queries = dot_f32(pick[...], tops[...]).astype(jnp.bfloat16)
    spare = jnp.zeros((lanes - rows, HEAD), jnp.bfloat16)
    score_rows = []
    for head in range(heads):
        cols = slice(head * HEAD, (head + 1) * HEAD)
        keys = jnp.concatenate([main_ref[1, :, cols], edge_ref[1, :, cols], spare], axis=0)
        scores = dot_f32(queries[:, cols], keys, 1) * inside[...]
        score_rows.append(jnp.sum(scores, axis=0, keepdims=True))
    scores = jnp.concatenate(score_rows + [jnp.zeros((8 - heads, lanes), jnp.float32)] * (heads < 8), axis=0)
    fore = back = scores
    for level in range(4):
        steps = 1 << level
        cut = cuts[level]
        fore = jnp.maximum(fore, ahead(fore, steps) + cut)
        back = jnp.maximum(back, pltpu.roll(back + cut, steps, 1))
    terms = jnp.exp((scores - jnp.maximum(fore, back)) * SCALE)
    fore = back = terms
    for level in range(4):
        steps = 1 << level
        keep = jnp.where(cuts[level] < 0.0, 0.0, 1.0)
        fore = fore + ahead(fore, steps) * keep
        back = back + pltpu.roll(back * keep, steps, 1)
    weights = terms / (fore + back - terms)
    for head in range(heads):
        cols = slice(head * HEAD, (head + 1) * HEAD)
        values = jnp.concatenate([main_ref[2, :, cols], edge_ref[2, :, cols], spare], axis=0)
        spread = (inside[...] * weights[head : head + 1]).astype(jnp.bfloat16)
        out_ref[head] = dot_f32(spread, values).astype(jnp.bfloat16)
    if joins:
        whole_ref[: heads] = earlier_ref[...]
        whole_ref[heads:] = out_ref[...]


def patch_states(place, bounds, parts, edge, slots, first_head, heads, earlier=None):
    byte_rows = parts.shape[1]
    rows = byte_rows + WIN
    lanes = -(-rows // 128) * 128
    width = heads * HEAD
    run = first_head // heads
    joins = earlier is not None
    states = jax.ShapeDtypeStruct((heads, slots, HEAD), jnp.bfloat16)
    states_spec = pl.BlockSpec((heads, slots, HEAD), lambda i: (0, 0, 0))
    whole = jax.ShapeDtypeStruct((2 * heads, slots, HEAD), jnp.bfloat16)
    whole_spec = pl.BlockSpec((2 * heads, slots, HEAD), lambda i: (0, 0, 0))
    return pl.pallas_call(
        functools.partial(patch_body, heads, joins),
        grid=(1,),
        in_specs=[
            pl.BlockSpec(memory_space=pltpu.SMEM),
            pl.BlockSpec(bounds.shape, lambda i: (0, 0)),
            pl.BlockSpec((3, byte_rows, width), lambda i: (0, 0, run)),
            pl.BlockSpec((3, WIN, width), lambda i: (0, 0, run)),
        ]
        + [states_spec] * joins,
        out_specs=[states_spec, whole_spec] if joins else states_spec,
        out_shape=[states, whole] if joins else states,
        scratch_shapes=[
            pltpu.VMEM((4, rows, HEAD), jnp.float32),
            pltpu.VMEM((4, 8, lanes), jnp.float32),
            pltpu.VMEM((slots, lanes), jnp.float32),
            pltpu.VMEM((slots, rows), jnp.bfloat16),
            pltpu.VMEM((rows, width), jnp.bfloat16),
        ],
        compiler_params=params(20),
        name="patch_states",
    )(place, bounds, parts, edge, *([earlier] if joins else []))


def column_block(width):
    return next(c for c in (512, 256, 128) if width % c == 0 and width > c)


def spread_states(states_refs, spread):
    slots = states_refs[0].shape[1]
    feature = lax.broadcasted_iota(jnp.int32, (HEAD, 2 * HEAD), 0)
    row = lax.broadcasted_iota(jnp.int32, (HEAD, 2 * HEAD), 1)
    for part in range(2):
        place = jnp.where(row == 2 * feature + part, 1.0, 0.0).astype(jnp.bfloat16)
        at = 0
        for states_ref in states_refs:
            for head in range(states_ref.shape[0]):
                spread[part * slots : (part + 1) * slots, at : at + 2 * HEAD] = dot_f32(
                    states_ref[head], place
                ).astype(jnp.bfloat16)
                at += 2 * HEAD


def project_body(half_ref, states_ref, weight_ref, sums_ref, held_ref, spread, blocks, arrived, held_arrived):
    count = states_ref.shape[0] * HEAD
    steps, _, _, block = blocks.shape
    half = half_ref[0]
    copies = [
        pltpu.make_async_copy(
            weight_ref.at[half_rows(half, count), :, pl.ds(step * block, block)],
            blocks.at[step],
            arrived.at[step],
        )
        for step in range(steps)
    ]
    hold = pltpu.make_async_copy(
        weight_ref.at[half_rows(1 - half, count), :, pl.ds(0, held_ref.shape[2])], held_ref, held_arrived
    )
    for copy in copies:
        copy.start()
    hold.start()
    spread_states([states_ref], spread)
    for step in range(steps):
        copies[step].wait()
        weights = blocks.at[step].reshape(2 * count, block)[...]
        sums_ref[:, step * block : (step + 1) * block] = dot_f32(spread[...], weights)
    hold.wait()


def half_rows(half, count):
    return pl.ds(pl.multiple_of(half * count, count), count)


def project(half, states, weight):
    heads, slots, _ = states.shape
    width = weight.shape[2]
    block = column_block(width)
    count = heads * HEAD
    in_vmem = pl.BlockSpec(memory_space=pltpu.VMEM)
    return pl.pallas_call(
        project_body,
        in_specs=[pl.BlockSpec(memory_space=pltpu.SMEM), in_vmem, pl.BlockSpec(memory_space=pl.ANY)],
        out_specs=[in_vmem, pl.BlockSpec(memory_space=pl.ANY)],
        out_shape=[
            jax.ShapeDtypeStruct((2 * slots, width), jnp.float32),
            pltpu.VMEM((count, 2, block), weight.dtype),
        ],
        scratch_shapes=[
            pltpu.VMEM((2 * slots, 2 * count), jnp.bfloat16),
            pltpu.VMEM((width // block, count, 2, block), jnp.bfloat16),
            pltpu.SemaphoreType.DMA((width // block,)),
            pltpu.SemaphoreType.DMA,
        ],
        compiler_params=params(28),
        cost_estimate=pl.CostEstimate(
            flops=8 * slots * count * width, bytes_accessed=8 * count * width, transcendentals=0
        ),
        name="project",
    )(half, states, weight)


def project_more_body(runs, half_ref, *refs):
    states_refs, (weight_ref, held_ref, before_ref, out_ref, spread, blocks, arrived) = refs[:runs], refs[runs:]
    slots = out_ref.shape[1]
    count = spread.shape[1] // 2
    later_steps, _, _, block = blocks.shape
    copies = [
        pltpu.make_async_copy(
            weight_ref.at[half_rows(half_ref[0], count), :, pl.ds((step + 1) * block, block)],
            blocks.at[step],
            arrived.at[step],
        )
        for step in range(later_steps)
    ]
    for copy in copies:
        copy.start()
    spread_states(states_refs, spread)
    for step in range(later_steps + 1):
        if step:
            copies[step - 1].wait()
        weights = (blocks.at[step - 1] if step else held_ref).reshape(2 * count, block)[...]
        before = before_ref[:, step * block : (step + 1) * block]
        total = (before + dot_f32(spread[...], weights)).astype(jnp.bfloat16)
        for part in range(block // HEAD):
            head = step * (block // HEAD) + part
            cols = slice(part * HEAD, (part + 1) * HEAD)
            out_ref[head, :, :HEAD] = total[:slots, cols]
            out_ref[head, :, HEAD:] = total[slots:, cols]


def project_more(half, states, weight, held, before):
    slots = states[0].shape[1]
    width = weight.shape[2]
    block = held.shape[2]
    later_steps = width // block - 1
    count = sum(run_states.shape[0] for run_states in states) * HEAD
    in_vmem = pl.BlockSpec(memory_space=pltpu.VMEM)
    return pl.pallas_call(
        functools.partial(project_more_body, len(states)),
        in_specs=[pl.BlockSpec(memory_space=pltpu.SMEM)]
        + [in_vmem] * len(states)
        + [pl.BlockSpec(memory_space=pl.ANY), in_vmem, in_vmem],
        out_specs=in_vmem,
        out_shape=jax.ShapeDtypeStruct((width // HEAD, slots, 2 * HEAD), jnp.bfloat16),
        scratch_shapes=[
            pltpu.VMEM((2 * slots, 2 * count), jnp.bfloat16),
            pltpu.VMEM((later_steps, count, 2, block), weight.dtype),
            pltpu.SemaphoreType.DMA((later_steps,)),
        ],
        compiler_params=params(28),
        cost_estimate=pl.CostEstimate(
            flops=8 * slots * count * width, bytes_accessed=4 * count * width, transcendentals=0
        ),
        name="project_more",
    )(half, *states, weight, pltpu.with_memory_space_constraint(held, pltpu.VMEM), before)


def attend_body(block, bias_ref, query_ref, kv_ref, out_ref, values, scores, terms):
    slots = kv_ref.shape[0]
    count = slots // block
    values[:, :HEAD] = kv_ref[:, HEAD:]
    values[:, HEAD:] = jnp.ones((slots, HEAD), jnp.bfloat16)
    row = lax.broadcasted_iota(jnp.int32, (block, block), 0)
    col = lax.broadcasted_iota(jnp.int32, (block, block), 1)
    later = jnp.where(col <= row, 0.0, MASKED)
    top = [None] * count

    def tile(index):
        return slice(index * block, (index + 1) * block)

    def score(at, index):
        found = dot_f32(query_ref[tile(at)], kv_ref[tile(index), :HEAD], 1) * SCALE_2 + bias_ref[:, tile(index)]
        if index == at:
            found = found + later
        scores[at % 2, :, tile(index)] = found
        for lane in range(0, block, 128):
            part = found[:, lane : lane + 128]
            top[at] = part if top[at] is None else jnp.maximum(top[at], part)
        if index == at:
            top[at] = jnp.max(top[at], axis=1, keepdims=True)

    def term(at, index):
        found = jnp.exp2(scores[at % 2, :, tile(index)] - top[at])
        high = found.astype(jnp.bfloat16)
        terms[at % 2, 0, :, tile(index)] = high
        terms[at % 2, 1, :, tile(index)] = (found - high.astype(jnp.float32)).astype(jnp.bfloat16)

    for at in range(-2, count):
        total = None
        for index in range(at + 3):
            if at + 1 < count and 0 <= at + 1 and index <= at + 1:
                term(at + 1, index)
            if 0 <= at and index <= at:
                part = dot_f32(terms[at % 2, 0, :, tile(index)], values[tile(index)]) + dot_f32(
                    terms[at % 2, 1, :, tile(index)], values[tile(index)]
                )
                total = part if total is None else total + part
            if at + 2 < count:
                score(at + 2, index)
        if 0 <= at:
            mixed = query_ref[tile(at)].astype(jnp.float32) + total[:, :HEAD] / total[:, HEAD:]
            out_ref[tile(at)] = mixed.astype(jnp.bfloat16)


def attend(bias, query, kv):
    slots = kv.shape[0]
    block = next(b for b in (256, 128) if slots % b == 0)
    return pl.pallas_call(
        functools.partial(attend_body, block),
        out_shape=jax.ShapeDtypeStruct((slots, HEAD), jnp.bfloat16),
        scratch_shapes=[
            pltpu.VMEM((slots, 2 * HEAD), jnp.bfloat16),
            pltpu.VMEM((2, block, slots), jnp.float32),
            pltpu.VMEM((2, 2, block, slots), jnp.bfloat16),
        ],
        compiler_params=params(28),
        name="attend",
    )(bias, query, kv)


def attend_gathered(place, valid, queries, keys, values):
    slots, width = queries.shape
    heads = width // HEAD
    keys = lax.all_gather(keys, "ctx", axis=0, tiled=True)
    values = lax.all_gather(values, "ctx", axis=0, tiled=True)
    total = keys.shape[0]
    query_slot = place * slots + jnp.arange(slots, dtype=jnp.int32)
    visible = (jnp.arange(total, dtype=jnp.int32)[None, :] <= query_slot[:, None]) & valid[None, :]
    scores = jnp.einsum(
        "qhd,khd->hqk",
        queries.reshape(slots, heads, HEAD),
        keys.reshape(total, heads, HEAD),
        preferred_element_type=jnp.float32,
    )
    scores = jnp.where(visible[None], scores * SCALE, MASKED)
    terms = jnp.where(visible[None], jnp.exp(scores - jnp.max(scores, axis=2, keepdims=True)), 0.0)
    sums = jnp.sum(terms, axis=2)
    attended = jnp.einsum(
        "hqk,khd->hqd",
        terms,
        values.reshape(total, heads, HEAD).astype(jnp.float32),
        precision=lax.Precision.HIGHEST,
    )
    attended = attended / jnp.where(sums > 0, sums, 1.0)[:, :, None]
    attended = attended.transpose(1, 0, 2).reshape(slots, width)
    return (queries.astype(jnp.float32) + attended).astype(jnp.bfloat16)


def shards(byte_qkv, kv_weight, patch_bounds):
    width = byte_qkv.shape[2]
    heads = width // HEAD
    slots = patch_bounds.shape[1] - 1
    ctx_count, mp_count = lax.axis_size("ctx"), lax.axis_size("mp")
    place = lax.axis_index("ctx").astype(jnp.int32)
    half = lax.axis_index("mp").astype(jnp.int32)

    edge = lax.ppermute(byte_qkv[:WIN], "ctx", [(i + 1, i) for i in range(ctx_count - 1)])
    parts = byte_qkv.transpose(1, 0, 2)
    edge = edge.transpose(1, 0, 2)
    in_hbm = functools.partial(pltpu.with_memory_space_constraint, memory_space=pltpu.HBM)
    byte_phase = functools.partial(
        patch_states, place[None], in_hbm(patch_bounds), in_hbm(parts), edge, slots
    )
    run = max(heads // 2, 1)
    first = byte_phase(0, run)
    states = first
    if heads > run:
        second, states = byte_phase(run, run, first)

    paired = ctx_count == heads
    if mp_count == 2:
        others = [lax.ppermute(run_states, "mp", [(0, 1), (1, 0)]) for run_states in (first, second)]
        before, held = project(half[None], states, kv_weight)
        other_half = 1 - half
    else:
        others = [lax.all_gather(states, "mp", axis=0, tiled=True)]
        before = jnp.zeros((2 * slots, width), jnp.float32)
        other_half = jnp.zeros_like(half)
        held = kv_weight[:, :, : column_block(width)]
    if paired:
        sent, others[0] = lax.optimization_barrier((states, others[0]))
        query = lax.all_to_all(sent, "ctx", 0, 0, tiled=True).reshape(ctx_count * slots, HEAD)
    kv = project_more(other_half[None], others, kv_weight, held, before)

    valid = patch_bounds[:, 1:] > patch_bounds[:, :-1]
    if paired:
        bias = jnp.where(valid, 0.0, MASKED).astype(jnp.float32).reshape(1, ctx_count * slots)
        kv = lax.all_to_all(kv, "ctx", 0, 0, tiled=True).reshape(ctx_count * slots, 2 * HEAD)
        mixed = attend(bias, query, kv).reshape(ctx_count, slots, HEAD)
        mixed = lax.all_to_all(mixed, "ctx", 0, 0, tiled=True)
        mixed = mixed.transpose(1, 0, 2).reshape(slots, width)
    else:
        query, keys, values = (
            part.transpose(1, 0, 2).reshape(slots, width)
            for part in (states, kv[:, :, :HEAD], kv[:, :, HEAD:])
        )
        mixed = attend_gathered(place, valid.reshape(-1), query, keys, values)
    live = lax.dynamic_index_in_dim(valid, place, 0, keepdims=False)
    return jnp.where(live[:, None], mixed, jnp.zeros_like(mixed))


def solution(mesh):
    return jax.shard_map(
        shards,
        mesh=mesh,
        in_specs=(P("ctx", None, "mp"), P(None, None, "mp"), P()),
        out_specs=P("ctx", "mp"),
        check_vma=False,
    )
```

```python
import functools
import math

import jax
import jax.numpy as jnp
from jax import lax
from jax.experimental import pallas as pl
from jax.experimental.pallas import tpu as pltpu
from jax.sharding import PartitionSpec as P

D = 4096
HEADS = 32
WIN = 16
HEAD = D // HEADS
SCALE = 1.0 / math.sqrt(HEAD)
SCALE_2 = SCALE * math.log2(math.e)
MASKED = -1e30


def params(mebibytes):
    return pltpu.CompilerParams(vmem_limit_bytes=mebibytes * 1024 * 1024)


def dot_f32(left, right, right_dim=0):
    return lax.dot_general(
        left, right, (((1,), (right_dim,)), ((), ())), preferred_element_type=jnp.float32
    )


def ahead(row, steps):
    return pltpu.roll(row, row.shape[1] - steps, 1)


def outline_body(place_ref, bounds_ref, parts_ref, held_ref, pens, cuts, inside, pick, arrived):
    load = pltpu.make_async_copy(parts_ref, held_ref, arrived)
    load.start()
    byte_rows = parts_ref.shape[1]
    slots, lanes = inside.shape
    rows = pens.shape[1]
    entries = bounds_ref.shape[1]
    place = place_ref[0]
    local = (bounds_ref[pl.ds(place, 1), :] - place * byte_rows).astype(jnp.float32)
    entry = lax.broadcasted_iota(jnp.int32, (slots, entries), 1)
    slot = lax.broadcasted_iota(jnp.int32, (slots, entries), 0)
    first = jnp.sum(jnp.where(entry == slot, local, 0.0), axis=1, keepdims=True)
    after = jnp.sum(jnp.where(entry == slot + 1, local, 0.0), axis=1, keepdims=True)
    byte = lax.broadcasted_iota(jnp.int32, (slots, lanes), 1).astype(jnp.float32)
    member = (byte >= first) & (byte < after)
    inside[...] = jnp.where(member, 1.0, 0.0)
    pick[...] = jnp.where(member & (byte == first), 1.0, 0.0)[:, :rows].astype(jnp.bfloat16)
    edges = jnp.where((byte == first) | (byte == after), 1.0, 0.0)
    cut = jnp.where(jnp.max(edges, axis=0, keepdims=True) > 0.0, -jnp.inf, 0.0)
    cut = ahead(jnp.broadcast_to(cut, (8, lanes)), 1)
    cuts[0] = cut
    at = lax.broadcasted_iota(jnp.int32, (rows, entries), 0).astype(jnp.float32)
    begins = jnp.max(jnp.where(at == local, 1.0, 0.0), axis=1, keepdims=True)
    pen = jnp.broadcast_to(jnp.where(begins > 0.0, -jnp.inf, 0.0), (rows, HEAD))
    pen = pltpu.roll(pen, rows - 1, 0)
    pens[0] = pen
    for level in range(1, 4):
        steps = 1 << (level - 1)
        cut = cut + ahead(cut, steps)
        cuts[level] = cut
        pen = pen + pltpu.roll(pen, rows - steps, 0)
        pens[level] = pen
    load.wait()


def outline(place, bounds, parts, slots):
    rows = parts.shape[1] + WIN
    lanes = -(-rows // 128) * 128
    in_vmem = pl.BlockSpec(memory_space=pltpu.VMEM)
    anywhere = pl.BlockSpec(memory_space=pl.ANY)
    found = pl.pallas_call(
        outline_body,
        in_specs=[pl.BlockSpec(memory_space=pltpu.SMEM), in_vmem, anywhere],
        out_specs=[anywhere] + [in_vmem] * 4,
        out_shape=[
            pltpu.VMEM(parts.shape, parts.dtype),
            pltpu.VMEM((4, rows, HEAD), jnp.float32),
            pltpu.VMEM((4, 8, lanes), jnp.float32),
            pltpu.VMEM((slots, lanes), jnp.float32),
            pltpu.VMEM((slots, rows), jnp.bfloat16),
        ],
        scratch_shapes=[pltpu.SemaphoreType.DMA],
        compiler_params=params(20),
        name="outline",
    )(place, bounds, parts)
    return [pltpu.with_memory_space_constraint(array, pltpu.VMEM) for array in found]


def patch_body(first_head, joins, main_ref, pens, cuts, inside, pick, edge_ref, *refs):
    if joins:
        earlier_ref, out_ref, whole_ref, tops = refs
    else:
        out_ref, tops = refs
    heads = out_ref.shape[0]
    rows = pens.shape[1]
    lanes = inside.shape[1]

    def head_cols(head):
        return slice((first_head + head) * HEAD, (first_head + head + 1) * HEAD)

    for head in range(heads):
        cols = head_cols(head)
        top = jnp.concatenate([main_ref[0, :, cols], edge_ref[0, :, cols]], axis=0).astype(jnp.float32)
        for level in range(4):
            top = jnp.maximum(top, pltpu.roll(top, rows - (1 << level), 0) + pens[level])
        tops[:, head * HEAD : (head + 1) * HEAD] = top.astype(jnp.bfloat16)
    queries = dot_f32(pick[...], tops[...]).astype(jnp.bfloat16)
    spare = jnp.zeros((lanes - rows, HEAD), jnp.bfloat16)
    score_rows = []
    for head in range(heads):
        cols = head_cols(head)
        keys = jnp.concatenate([main_ref[1, :, cols], edge_ref[1, :, cols], spare], axis=0)
        scores = dot_f32(queries[:, head * HEAD : (head + 1) * HEAD], keys, 1) * inside[...]
        score_rows.append(jnp.sum(scores, axis=0, keepdims=True))
    scores = jnp.concatenate(score_rows + [jnp.zeros((8 - heads, lanes), jnp.float32)] * (heads < 8), axis=0)
    fore = back = scores
    for level in range(4):
        steps = 1 << level
        cut = cuts[level]
        fore = jnp.maximum(fore, ahead(fore, steps) + cut)
        back = jnp.maximum(back, pltpu.roll(back + cut, steps, 1))
    terms = jnp.exp((scores - jnp.maximum(fore, back)) * SCALE)
    fore = back = terms
    for level in range(4):
        steps = 1 << level
        keep = jnp.where(cuts[level] < 0.0, 0.0, 1.0)
        fore = fore + ahead(fore, steps) * keep
        back = back + pltpu.roll(back * keep, steps, 1)
    weights = terms / (fore + back - terms)
    for head in range(heads):
        cols = head_cols(head)
        values = jnp.concatenate([main_ref[2, :, cols], edge_ref[2, :, cols], spare], axis=0)
        spread = (inside[...] * weights[head : head + 1]).astype(jnp.bfloat16)
        out_ref[head] = dot_f32(spread, values).astype(jnp.bfloat16)
    if joins:
        whole_ref[: heads] = earlier_ref[...]
        whole_ref[heads:] = out_ref[...]


def patch_states(found, edge, first_head, heads, earlier=None):
    slots, rows = found[-1].shape
    joins = earlier is not None
    states = jax.ShapeDtypeStruct((heads, slots, HEAD), jnp.bfloat16)
    whole = jax.ShapeDtypeStruct((2 * heads, slots, HEAD), jnp.bfloat16)
    in_vmem = pl.BlockSpec(memory_space=pltpu.VMEM)
    return pl.pallas_call(
        functools.partial(patch_body, first_head, joins),
        in_specs=[in_vmem] * (len(found) + 1 + joins),
        out_specs=[in_vmem, in_vmem] if joins else in_vmem,
        out_shape=[states, whole] if joins else states,
        scratch_shapes=[pltpu.VMEM((rows, heads * HEAD), jnp.bfloat16)],
        compiler_params=params(20),
        name="patch_states",
    )(*found, edge, *([earlier] if joins else []))


def column_block(width):
    return next(c for c in (512, 256, 128) if width % c == 0 and width > c)


def spread_states(states_refs, spread):
    slots = states_refs[0].shape[1]
    feature = lax.broadcasted_iota(jnp.int32, (HEAD, 2 * HEAD), 0)
    row = lax.broadcasted_iota(jnp.int32, (HEAD, 2 * HEAD), 1)
    for part in range(2):
        place = jnp.where(row == 2 * feature + part, 1.0, 0.0).astype(jnp.bfloat16)
        at = 0
        for states_ref in states_refs:
            for head in range(states_ref.shape[0]):
                spread[part * slots : (part + 1) * slots, at : at + 2 * HEAD] = dot_f32(
                    states_ref[head], place
                ).astype(jnp.bfloat16)
                at += 2 * HEAD


def project_body(half_ref, states_ref, weight_ref, sums_ref, held_ref, spread, blocks, arrived, held_arrived):
    count = states_ref.shape[0] * HEAD
    steps, _, _, block = blocks.shape
    half = half_ref[0]
    copies = [
        pltpu.make_async_copy(
            weight_ref.at[half_rows(half, count), :, pl.ds(step * block, block)],
            blocks.at[step],
            arrived.at[step],
        )
        for step in range(steps)
    ]
    hold = pltpu.make_async_copy(
        weight_ref.at[half_rows(1 - half, count), :, pl.ds(0, held_ref.shape[2])], held_ref, held_arrived
    )
    for copy in copies:
        copy.start()
    hold.start()
    spread_states([states_ref], spread)
    for step in range(steps):
        copies[step].wait()
        weights = blocks.at[step].reshape(2 * count, block)[...]
        sums_ref[:, step * block : (step + 1) * block] = dot_f32(spread[...], weights)
    hold.wait()


def half_rows(half, count):
    return pl.ds(pl.multiple_of(half * count, count), count)


def project(half, states, weight):
    heads, slots, _ = states.shape
    width = weight.shape[2]
    block = column_block(width)
    count = heads * HEAD
    in_vmem = pl.BlockSpec(memory_space=pltpu.VMEM)
    return pl.pallas_call(
        project_body,
        in_specs=[pl.BlockSpec(memory_space=pltpu.SMEM), in_vmem, pl.BlockSpec(memory_space=pl.ANY)],
        out_specs=[in_vmem, pl.BlockSpec(memory_space=pl.ANY)],
        out_shape=[
            jax.ShapeDtypeStruct((2 * slots, width), jnp.float32),
            pltpu.VMEM((count, 2, block), weight.dtype),
        ],
        scratch_shapes=[
            pltpu.VMEM((2 * slots, 2 * count), jnp.bfloat16),
            pltpu.VMEM((width // block, count, 2, block), jnp.bfloat16),
            pltpu.SemaphoreType.DMA((width // block,)),
            pltpu.SemaphoreType.DMA,
        ],
        compiler_params=params(28),
        cost_estimate=pl.CostEstimate(
            flops=8 * slots * count * width, bytes_accessed=8 * count * width, transcendentals=0
        ),
        name="project",
    )(half, states, weight)


def project_more_body(runs, half_ref, *refs):
    states_refs, (weight_ref, held_ref, before_ref, out_ref, spread, blocks, arrived) = refs[:runs], refs[runs:]
    slots = out_ref.shape[1]
    count = spread.shape[1] // 2
    later_steps, _, _, block = blocks.shape
    copies = [
        pltpu.make_async_copy(
            weight_ref.at[half_rows(half_ref[0], count), :, pl.ds((step + 1) * block, block)],
            blocks.at[step],
            arrived.at[step],
        )
        for step in range(later_steps)
    ]
    for copy in copies:
        copy.start()
    spread_states(states_refs, spread)
    for step in range(later_steps + 1):
        if step:
            copies[step - 1].wait()
        weights = (blocks.at[step - 1] if step else held_ref).reshape(2 * count, block)[...]
        before = before_ref[:, step * block : (step + 1) * block]
        total = (before + dot_f32(spread[...], weights)).astype(jnp.bfloat16)
        for part in range(block // HEAD):
            head = step * (block // HEAD) + part
            cols = slice(part * HEAD, (part + 1) * HEAD)
            out_ref[head, :, :HEAD] = total[:slots, cols]
            out_ref[head, :, HEAD:] = total[slots:, cols]


def project_more(half, states, weight, held, before):
    slots = states[0].shape[1]
    width = weight.shape[2]
    block = held.shape[2]
    later_steps = width // block - 1
    count = sum(run_states.shape[0] for run_states in states) * HEAD
    in_vmem = pl.BlockSpec(memory_space=pltpu.VMEM)
    return pl.pallas_call(
        functools.partial(project_more_body, len(states)),
        in_specs=[pl.BlockSpec(memory_space=pltpu.SMEM)]
        + [in_vmem] * len(states)
        + [pl.BlockSpec(memory_space=pl.ANY), in_vmem, in_vmem],
        out_specs=in_vmem,
        out_shape=jax.ShapeDtypeStruct((width // HEAD, slots, 2 * HEAD), jnp.bfloat16),
        scratch_shapes=[
            pltpu.VMEM((2 * slots, 2 * count), jnp.bfloat16),
            pltpu.VMEM((later_steps, count, 2, block), weight.dtype),
            pltpu.SemaphoreType.DMA((later_steps,)),
        ],
        compiler_params=params(28),
        cost_estimate=pl.CostEstimate(
            flops=8 * slots * count * width, bytes_accessed=4 * count * width, transcendentals=0
        ),
        name="project_more",
    )(half, *states, weight, pltpu.with_memory_space_constraint(held, pltpu.VMEM), before)


def attend_body(block, bias_ref, query_ref, kv_ref, out_ref, values, scores, terms):
    slots = kv_ref.shape[0]
    count = slots // block
    values[:, :HEAD] = kv_ref[:, HEAD:]
    values[:, HEAD:] = jnp.ones((slots, HEAD), jnp.bfloat16)
    row = lax.broadcasted_iota(jnp.int32, (block, block), 0)
    col = lax.broadcasted_iota(jnp.int32, (block, block), 1)
    later = jnp.where(col <= row, 0.0, MASKED)
    top = [None] * count

    def tile(index):
        return slice(index * block, (index + 1) * block)

    def score(at, index):
        found = dot_f32(query_ref[tile(at)], kv_ref[tile(index), :HEAD], 1) * SCALE_2 + bias_ref[:, tile(index)]
        if index == at:
            found = found + later
        scores[at % 2, :, tile(index)] = found
        for lane in range(0, block, 128):
            part = found[:, lane : lane + 128]
            top[at] = part if top[at] is None else jnp.maximum(top[at], part)
        if index == at:
            top[at] = jnp.max(top[at], axis=1, keepdims=True)

    def term(at, index):
        found = jnp.exp2(scores[at % 2, :, tile(index)] - top[at])
        high = found.astype(jnp.bfloat16)
        terms[at % 2, 0, :, tile(index)] = high
        terms[at % 2, 1, :, tile(index)] = (found - high.astype(jnp.float32)).astype(jnp.bfloat16)

    for at in range(-2, count):
        total = None
        for index in range(at + 3):
            if at + 1 < count and 0 <= at + 1 and index <= at + 1:
                term(at + 1, index)
            if 0 <= at and index <= at:
                part = dot_f32(terms[at % 2, 0, :, tile(index)], values[tile(index)]) + dot_f32(
                    terms[at % 2, 1, :, tile(index)], values[tile(index)]
                )
                total = part if total is None else total + part
            if at + 2 < count:
                score(at + 2, index)
        if 0 <= at:
            mixed = query_ref[tile(at)].astype(jnp.float32) + total[:, :HEAD] / total[:, HEAD:]
            out_ref[tile(at)] = mixed.astype(jnp.bfloat16)


def attend(bias, query, kv):
    slots = kv.shape[0]
    block = next(b for b in (256, 128) if slots % b == 0)
    return pl.pallas_call(
        functools.partial(attend_body, block),
        out_shape=jax.ShapeDtypeStruct((slots, HEAD), jnp.bfloat16),
        scratch_shapes=[
            pltpu.VMEM((slots, 2 * HEAD), jnp.bfloat16),
            pltpu.VMEM((2, block, slots), jnp.float32),
            pltpu.VMEM((2, 2, block, slots), jnp.bfloat16),
        ],
        compiler_params=params(28),
        name="attend",
    )(bias, query, kv)


def attend_gathered(place, valid, queries, keys, values):
    slots, width = queries.shape
    heads = width // HEAD
    keys = lax.all_gather(keys, "ctx", axis=0, tiled=True)
    values = lax.all_gather(values, "ctx", axis=0, tiled=True)
    total = keys.shape[0]
    query_slot = place * slots + jnp.arange(slots, dtype=jnp.int32)
    visible = (jnp.arange(total, dtype=jnp.int32)[None, :] <= query_slot[:, None]) & valid[None, :]
    scores = jnp.einsum(
        "qhd,khd->hqk",
        queries.reshape(slots, heads, HEAD),
        keys.reshape(total, heads, HEAD),
        preferred_element_type=jnp.float32,
    )
    scores = jnp.where(visible[None], scores * SCALE, MASKED)
    terms = jnp.where(visible[None], jnp.exp(scores - jnp.max(scores, axis=2, keepdims=True)), 0.0)
    sums = jnp.sum(terms, axis=2)
    attended = jnp.einsum(
        "hqk,khd->hqd",
        terms,
        values.reshape(total, heads, HEAD).astype(jnp.float32),
        precision=lax.Precision.HIGHEST,
    )
    attended = attended / jnp.where(sums > 0, sums, 1.0)[:, :, None]
    attended = attended.transpose(1, 0, 2).reshape(slots, width)
    return (queries.astype(jnp.float32) + attended).astype(jnp.bfloat16)


def shards(byte_qkv, kv_weight, patch_bounds):
    width = byte_qkv.shape[2]
    heads = width // HEAD
    slots = patch_bounds.shape[1] - 1
    ctx_count, mp_count = lax.axis_size("ctx"), lax.axis_size("mp")
    place = lax.axis_index("ctx").astype(jnp.int32)
    half = lax.axis_index("mp").astype(jnp.int32)

    edge = lax.ppermute(byte_qkv[:WIN], "ctx", [(i + 1, i) for i in range(ctx_count - 1)])
    parts = byte_qkv.transpose(1, 0, 2)
    edge = edge.transpose(1, 0, 2)
    in_hbm = functools.partial(pltpu.with_memory_space_constraint, memory_space=pltpu.HBM)
    found = outline(place[None], in_hbm(patch_bounds), in_hbm(parts), slots)
    byte_phase = functools.partial(patch_states, found, edge)
    run = max(heads // 2, 1)
    first = byte_phase(0, run)
    states = first
    if heads > run:
        second, states = byte_phase(run, run, first)

    paired = ctx_count == heads
    if mp_count == 2:
        others = [lax.ppermute(run_states, "mp", [(0, 1), (1, 0)]) for run_states in (first, second)]
        before, held = project(half[None], states, kv_weight)
        other_half = 1 - half
    else:
        others = [lax.all_gather(states, "mp", axis=0, tiled=True)]
        before = jnp.zeros((2 * slots, width), jnp.float32)
        other_half = jnp.zeros_like(half)
        held = kv_weight[:, :, : column_block(width)]
    if paired:
        sent, others[0] = lax.optimization_barrier((states, others[0]))
        query = lax.all_to_all(sent, "ctx", 0, 0, tiled=True).reshape(ctx_count * slots, HEAD)
    kv = project_more(other_half[None], others, kv_weight, held, before)

    valid = patch_bounds[:, 1:] > patch_bounds[:, :-1]
    if paired:
        bias = jnp.where(valid, 0.0, MASKED).astype(jnp.float32).reshape(1, ctx_count * slots)
        kv = lax.all_to_all(kv, "ctx", 0, 0, tiled=True).reshape(ctx_count * slots, 2 * HEAD)
        mixed = attend(bias, query, kv).reshape(ctx_count, slots, HEAD)
        mixed = lax.all_to_all(mixed, "ctx", 0, 0, tiled=True)
        mixed = mixed.transpose(1, 0, 2).reshape(slots, width)
    else:
        query, keys, values = (
            part.transpose(1, 0, 2).reshape(slots, width)
            for part in (states, kv[:, :, :HEAD], kv[:, :, HEAD:])
        )
        mixed = attend_gathered(place, valid.reshape(-1), query, keys, values)
    live = lax.dynamic_index_in_dim(valid, place, 0, keepdims=False)
    return jnp.where(live[:, None], mixed, jnp.zeros_like(mixed))


def solution(mesh):
    return jax.shard_map(
        shards,
        mesh=mesh,
        in_specs=(P("ctx", None, "mp"), P(None, None, "mp"), P()),
        out_specs=P("ctx", "mp"),
        check_vma=False,
    )
```

```python
import functools
import math

import jax
import jax.numpy as jnp
from jax import lax
from jax.experimental import pallas as pl
from jax.experimental.pallas import tpu as pltpu
from jax.sharding import PartitionSpec as P

D = 4096
HEADS = 32
WIN = 16
HEAD = D // HEADS
SCALE = 1.0 / math.sqrt(HEAD)
SCALE_2 = SCALE * math.log2(math.e)
MASKED = -1e30


def params(mebibytes):
    return pltpu.CompilerParams(vmem_limit_bytes=mebibytes * 1024 * 1024)


def dot_f32(left, right, right_dim=0):
    return lax.dot_general(
        left, right, (((1,), (right_dim,)), ((), ())), preferred_element_type=jnp.float32
    )


def ahead(row, steps):
    return pltpu.roll(row, row.shape[1] - steps, 1)


def outline_body(place_ref, bounds_ref, parts_ref, held_ref, pens, cuts, inside, pick, arrived):
    load = pltpu.make_async_copy(parts_ref, held_ref, arrived)
    load.start()
    byte_rows = parts_ref.shape[1]
    slots, lanes = inside.shape
    rows = pens.shape[1]
    entries = bounds_ref.shape[1]
    place = place_ref[0]
    local = (bounds_ref[pl.ds(place, 1), :] - place * byte_rows).astype(jnp.float32)
    entry = lax.broadcasted_iota(jnp.int32, (slots, entries), 1)
    slot = lax.broadcasted_iota(jnp.int32, (slots, entries), 0)
    first = jnp.sum(jnp.where(entry == slot, local, 0.0), axis=1, keepdims=True)
    after = jnp.sum(jnp.where(entry == slot + 1, local, 0.0), axis=1, keepdims=True)
    byte = lax.broadcasted_iota(jnp.int32, (slots, lanes), 1).astype(jnp.float32)
    member = (byte >= first) & (byte < after)
    inside[...] = jnp.where(member, 1.0, 0.0)
    pick[...] = jnp.where(member & (byte == first), 1.0, 0.0)[:, :rows].astype(jnp.bfloat16)
    edges = jnp.where((byte == first) | (byte == after), 1.0, 0.0)
    cut = jnp.where(jnp.max(edges, axis=0, keepdims=True) > 0.0, -jnp.inf, 0.0)
    cut = ahead(jnp.broadcast_to(cut, (8, lanes)), 1)
    cuts[0] = cut
    at = lax.broadcasted_iota(jnp.int32, (rows, entries), 0).astype(jnp.float32)
    begins = jnp.max(jnp.where(at == local, 1.0, 0.0), axis=1, keepdims=True)
    pen = jnp.broadcast_to(jnp.where(begins > 0.0, -jnp.inf, 0.0), (rows, HEAD))
    pen = pltpu.roll(pen, rows - 1, 0)
    pens[0] = pen
    for level in range(1, 4):
        steps = 1 << (level - 1)
        cut = cut + ahead(cut, steps)
        cuts[level] = cut
        pen = pen + pltpu.roll(pen, rows - steps, 0)
        pens[level] = pen
    load.wait()


def outline(place, bounds, parts, slots):
    rows = parts.shape[1] + WIN
    lanes = -(-rows // 128) * 128
    in_vmem = pl.BlockSpec(memory_space=pltpu.VMEM)
    anywhere = pl.BlockSpec(memory_space=pl.ANY)
    found = pl.pallas_call(
        outline_body,
        in_specs=[pl.BlockSpec(memory_space=pltpu.SMEM), in_vmem, anywhere],
        out_specs=[anywhere] + [in_vmem] * 4,
        out_shape=[
            pltpu.VMEM(parts.shape, parts.dtype),
            pltpu.VMEM((4, rows, HEAD), jnp.float32),
            pltpu.VMEM((4, 8, lanes), jnp.float32),
            pltpu.VMEM((slots, lanes), jnp.float32),
            pltpu.VMEM((slots, rows), jnp.bfloat16),
        ],
        scratch_shapes=[pltpu.SemaphoreType.DMA],
        compiler_params=params(20),
        name="outline",
    )(place, bounds, parts)
    return [pltpu.with_memory_space_constraint(array, pltpu.VMEM) for array in found]


def patch_body(first_head, joins, main_ref, pens, cuts, inside, pick, edge_ref, *refs):
    if joins:
        lead_ref, rest_ref, out_ref, whole_ref, tops = refs
        held_back = rest_ref.shape[0]
        heads = out_ref.shape[0] - held_back
    else:
        lead_ref, rest_ref, tops = refs
        held_back = 0
        heads = lead_ref.shape[0] + rest_ref.shape[0]
    rows = pens.shape[1]
    lanes = inside.shape[1]

    def head_cols(head):
        return slice((first_head + head) * HEAD, (first_head + head + 1) * HEAD)

    for head in range(heads):
        cols = head_cols(head)
        top = jnp.concatenate([main_ref[0, :, cols], edge_ref[0, :, cols]], axis=0).astype(jnp.float32)
        for level in range(4):
            top = jnp.maximum(top, pltpu.roll(top, rows - (1 << level), 0) + pens[level])
        tops[:, head * HEAD : (head + 1) * HEAD] = top.astype(jnp.bfloat16)
    queries = dot_f32(pick[...], tops[...]).astype(jnp.bfloat16)
    spare = jnp.zeros((lanes - rows, HEAD), jnp.bfloat16)
    score_rows = []
    for head in range(heads):
        cols = head_cols(head)
        keys = jnp.concatenate([main_ref[1, :, cols], edge_ref[1, :, cols], spare], axis=0)
        scores = dot_f32(queries[:, head * HEAD : (head + 1) * HEAD], keys, 1) * inside[...]
        score_rows.append(jnp.sum(scores, axis=0, keepdims=True))
    scores = jnp.concatenate(score_rows + [jnp.zeros((8 - heads, lanes), jnp.float32)] * (heads < 8), axis=0)
    fore = back = scores
    for level in range(4):
        steps = 1 << level
        cut = cuts[level]
        fore = jnp.maximum(fore, ahead(fore, steps) + cut)
        back = jnp.maximum(back, pltpu.roll(back + cut, steps, 1))
    terms = jnp.exp((scores - jnp.maximum(fore, back)) * SCALE)
    fore = back = terms
    for level in range(4):
        steps = 1 << level
        keep = jnp.where(cuts[level] < 0.0, 0.0, 1.0)
        fore = fore + ahead(fore, steps) * keep
        back = back + pltpu.roll(back * keep, steps, 1)
    weights = terms / (fore + back - terms)
    for head in range(heads):
        cols = head_cols(head)
        values = jnp.concatenate([main_ref[2, :, cols], edge_ref[2, :, cols], spare], axis=0)
        spread = (inside[...] * weights[head : head + 1]).astype(jnp.bfloat16)
        states = dot_f32(spread, values).astype(jnp.bfloat16)
        if joins:
            out_ref[held_back + head] = states
        elif head < lead_ref.shape[0]:
            lead_ref[head] = states
        else:
            rest_ref[head - lead_ref.shape[0]] = states
    if joins:
        out_ref[:held_back] = rest_ref[...]
        whole_ref[: lead_ref.shape[0]] = lead_ref[...]
        whole_ref[lead_ref.shape[0] :] = out_ref[...]


def patch_states(found, edge, first_head, heads, earlier=()):
    slots, rows = found[-1].shape
    if earlier:
        counts = (earlier[1].shape[0] + heads, first_head + heads)
    else:
        lead = max(heads * 5 // 8, 1)
        counts = (lead, heads - lead)
    in_vmem = pl.BlockSpec(memory_space=pltpu.VMEM)
    return pl.pallas_call(
        functools.partial(patch_body, first_head, bool(earlier)),
        in_specs=[in_vmem] * (len(found) + 1 + len(earlier)),
        out_specs=[in_vmem, in_vmem],
        out_shape=[jax.ShapeDtypeStruct((count, slots, HEAD), jnp.bfloat16) for count in counts],
        scratch_shapes=[pltpu.VMEM((rows, heads * HEAD), jnp.bfloat16)],
        compiler_params=params(20),
        name="patch_states",
    )(*found, edge, *earlier)


def column_block(width):
    return next(c for c in (512, 256, 128) if width % c == 0 and width > c)


def spread_states(states_refs, spread):
    slots = states_refs[0].shape[1]
    feature = lax.broadcasted_iota(jnp.int32, (HEAD, 2 * HEAD), 0)
    row = lax.broadcasted_iota(jnp.int32, (HEAD, 2 * HEAD), 1)
    for part in range(2):
        place = jnp.where(row == 2 * feature + part, 1.0, 0.0).astype(jnp.bfloat16)
        at = 0
        for states_ref in states_refs:
            for head in range(states_ref.shape[0]):
                spread[part * slots : (part + 1) * slots, at : at + 2 * HEAD] = dot_f32(
                    states_ref[head], place
                ).astype(jnp.bfloat16)
                at += 2 * HEAD


def project_body(half_ref, states_ref, weight_ref, sums_ref, held_ref, spread, blocks, arrived, held_arrived):
    count = states_ref.shape[0] * HEAD
    steps, _, _, block = blocks.shape
    half = half_ref[0]
    copies = [
        pltpu.make_async_copy(
            weight_ref.at[half_rows(half, count), :, pl.ds(step * block, block)],
            blocks.at[step],
            arrived.at[step],
        )
        for step in range(1, steps)
    ]
    near = count // 2
    starts = [
        pltpu.make_async_copy(
            weight_ref.at[pl.ds(pl.multiple_of(half * count + part * near, near), near), :, pl.ds(0, block)],
            blocks.at[0, pl.ds(part * near, near)],
            arrived.at[part * steps],
        )
        for part in range(2)
    ]
    hold = pltpu.make_async_copy(
        weight_ref.at[half_rows(1 - half, count), :, pl.ds(0, held_ref.shape[2])], held_ref, held_arrived
    )
    for copy in starts + copies:
        copy.start()
    hold.start()
    spread_states([states_ref], spread)
    weights = blocks.at[0].reshape(2 * count, block)
    starts[0].wait()
    product = dot_f32(spread[:, :count], weights[:count])
    starts[1].wait()
    sums_ref[:, :block] = product + dot_f32(spread[:, count:], weights[count:])
    for step in range(1, steps):
        copies[step - 1].wait()
        weights = blocks.at[step].reshape(2 * count, block)[...]
        sums_ref[:, step * block : (step + 1) * block] = dot_f32(spread[...], weights)
    hold.wait()


def half_rows(half, count):
    return pl.ds(pl.multiple_of(half * count, count), count)


def project(half, states, weight):
    heads, slots, _ = states.shape
    width = weight.shape[2]
    block = column_block(width)
    count = heads * HEAD
    in_vmem = pl.BlockSpec(memory_space=pltpu.VMEM)
    return pl.pallas_call(
        project_body,
        in_specs=[pl.BlockSpec(memory_space=pltpu.SMEM), in_vmem, pl.BlockSpec(memory_space=pl.ANY)],
        out_specs=[in_vmem, pl.BlockSpec(memory_space=pl.ANY)],
        out_shape=[
            jax.ShapeDtypeStruct((2 * slots, width), jnp.float32),
            pltpu.VMEM((count, 2, block), weight.dtype),
        ],
        scratch_shapes=[
            pltpu.VMEM((2 * slots, 2 * count), jnp.bfloat16),
            pltpu.VMEM((width // block, count, 2, block), jnp.bfloat16),
            pltpu.SemaphoreType.DMA((width // block + 1,)),
            pltpu.SemaphoreType.DMA,
        ],
        compiler_params=params(28),
        cost_estimate=pl.CostEstimate(
            flops=8 * slots * count * width, bytes_accessed=8 * count * width, transcendentals=0
        ),
        name="project",
    )(half, states, weight)


def project_more_body(runs, half_ref, *refs):
    states_refs, (weight_ref, held_ref, before_ref, out_ref, spread, blocks, arrived) = refs[:runs], refs[runs:]
    slots = out_ref.shape[1]
    count = spread.shape[1] // 2
    later_steps, _, _, block = blocks.shape
    copies = [
        pltpu.make_async_copy(
            weight_ref.at[half_rows(half_ref[0], count), :, pl.ds((step + 1) * block, block)],
            blocks.at[step],
            arrived.at[step],
        )
        for step in range(later_steps)
    ]
    for copy in copies:
        copy.start()
    spread_states(states_refs, spread)
    for step in range(later_steps + 1):
        if step:
            copies[step - 1].wait()
        weights = (blocks.at[step - 1] if step else held_ref).reshape(2 * count, block)[...]
        before = before_ref[:, step * block : (step + 1) * block]
        total = (before + dot_f32(spread[...], weights)).astype(jnp.bfloat16)
        for part in range(block // HEAD):
            head = step * (block // HEAD) + part
            cols = slice(part * HEAD, (part + 1) * HEAD)
            out_ref[head, :, :HEAD] = total[:slots, cols]
            out_ref[head, :, HEAD:] = total[slots:, cols]


def project_more(half, states, weight, held, before):
    slots = states[0].shape[1]
    width = weight.shape[2]
    block = held.shape[2]
    later_steps = width // block - 1
    count = sum(run_states.shape[0] for run_states in states) * HEAD
    in_vmem = pl.BlockSpec(memory_space=pltpu.VMEM)
    return pl.pallas_call(
        functools.partial(project_more_body, len(states)),
        in_specs=[pl.BlockSpec(memory_space=pltpu.SMEM)]
        + [in_vmem] * len(states)
        + [pl.BlockSpec(memory_space=pl.ANY), in_vmem, in_vmem],
        out_specs=in_vmem,
        out_shape=jax.ShapeDtypeStruct((width // HEAD, slots, 2 * HEAD), jnp.bfloat16),
        scratch_shapes=[
            pltpu.VMEM((2 * slots, 2 * count), jnp.bfloat16),
            pltpu.VMEM((later_steps, count, 2, block), weight.dtype),
            pltpu.SemaphoreType.DMA((later_steps,)),
        ],
        compiler_params=params(28),
        cost_estimate=pl.CostEstimate(
            flops=8 * slots * count * width, bytes_accessed=4 * count * width, transcendentals=0
        ),
        name="project_more",
    )(half, *states, weight, pltpu.with_memory_space_constraint(held, pltpu.VMEM), before)


def attend_body(block, bias_ref, query_ref, kv_ref, out_ref, values, scores, terms):
    slots = kv_ref.shape[0]
    count = slots // block
    values[:, :HEAD] = kv_ref[:, HEAD:]
    values[:, HEAD:] = jnp.ones((slots, HEAD), jnp.bfloat16)
    row = lax.broadcasted_iota(jnp.int32, (block, block), 0)
    col = lax.broadcasted_iota(jnp.int32, (block, block), 1)
    later = jnp.where(col <= row, 0.0, MASKED)
    top = [None] * count

    def tile(index):
        return slice(index * block, (index + 1) * block)

    def score(at, index):
        found = dot_f32(query_ref[tile(at)], kv_ref[tile(index), :HEAD], 1) * SCALE_2 + bias_ref[:, tile(index)]
        if index == at:
            found = found + later
        scores[at % 2, :, tile(index)] = found
        for lane in range(0, block, 128):
            part = found[:, lane : lane + 128]
            top[at] = part if top[at] is None else jnp.maximum(top[at], part)
        if index == at:
            top[at] = jnp.max(top[at], axis=1, keepdims=True)

    def term(at, index):
        found = jnp.exp2(scores[at % 2, :, tile(index)] - top[at])
        high = found.astype(jnp.bfloat16)
        terms[at % 2, 0, :, tile(index)] = high
        terms[at % 2, 1, :, tile(index)] = (found - high.astype(jnp.float32)).astype(jnp.bfloat16)

    for at in range(-2, count):
        total = None
        for index in range(at + 3):
            if at + 1 < count and 0 <= at + 1 and index <= at + 1:
                term(at + 1, index)
            if 0 <= at and index <= at:
                part = dot_f32(terms[at % 2, 0, :, tile(index)], values[tile(index)]) + dot_f32(
                    terms[at % 2, 1, :, tile(index)], values[tile(index)]
                )
                total = part if total is None else total + part
            if at + 2 < count:
                score(at + 2, index)
        if 0 <= at:
            mixed = query_ref[tile(at)].astype(jnp.float32) + total[:, :HEAD] / total[:, HEAD:]
            out_ref[tile(at)] = mixed.astype(jnp.bfloat16)


def attend(bias, query, kv):
    slots = kv.shape[0]
    block = next(b for b in (256, 128) if slots % b == 0)
    return pl.pallas_call(
        functools.partial(attend_body, block),
        out_shape=jax.ShapeDtypeStruct((slots, HEAD), jnp.bfloat16),
        scratch_shapes=[
            pltpu.VMEM((slots, 2 * HEAD), jnp.bfloat16),
            pltpu.VMEM((2, block, slots), jnp.float32),
            pltpu.VMEM((2, 2, block, slots), jnp.bfloat16),
        ],
        compiler_params=params(28),
        name="attend",
    )(bias, query, kv)


def attend_gathered(place, valid, queries, keys, values):
    slots, width = queries.shape
    heads = width // HEAD
    keys = lax.all_gather(keys, "ctx", axis=0, tiled=True)
    values = lax.all_gather(values, "ctx", axis=0, tiled=True)
    total = keys.shape[0]
    query_slot = place * slots + jnp.arange(slots, dtype=jnp.int32)
    visible = (jnp.arange(total, dtype=jnp.int32)[None, :] <= query_slot[:, None]) & valid[None, :]
    scores = jnp.einsum(
        "qhd,khd->hqk",
        queries.reshape(slots, heads, HEAD),
        keys.reshape(total, heads, HEAD),
        preferred_element_type=jnp.float32,
    )
    scores = jnp.where(visible[None], scores * SCALE, MASKED)
    terms = jnp.where(visible[None], jnp.exp(scores - jnp.max(scores, axis=2, keepdims=True)), 0.0)
    sums = jnp.sum(terms, axis=2)
    attended = jnp.einsum(
        "hqk,khd->hqd",
        terms,
        values.reshape(total, heads, HEAD).astype(jnp.float32),
        precision=lax.Precision.HIGHEST,
    )
    attended = attended / jnp.where(sums > 0, sums, 1.0)[:, :, None]
    attended = attended.transpose(1, 0, 2).reshape(slots, width)
    return (queries.astype(jnp.float32) + attended).astype(jnp.bfloat16)


def shards(byte_qkv, kv_weight, patch_bounds):
    width = byte_qkv.shape[2]
    heads = width // HEAD
    slots = patch_bounds.shape[1] - 1
    ctx_count, mp_count = lax.axis_size("ctx"), lax.axis_size("mp")
    place = lax.axis_index("ctx").astype(jnp.int32)
    half = lax.axis_index("mp").astype(jnp.int32)

    edge = lax.ppermute(byte_qkv[:WIN], "ctx", [(i + 1, i) for i in range(ctx_count - 1)])
    parts = byte_qkv.transpose(1, 0, 2)
    edge = edge.transpose(1, 0, 2)
    in_hbm = functools.partial(pltpu.with_memory_space_constraint, memory_space=pltpu.HBM)
    found = outline(place[None], in_hbm(patch_bounds), in_hbm(parts), slots)
    byte_phase = functools.partial(patch_states, found, edge)
    run = heads // 2
    first = byte_phase(0, run)
    rest, states = byte_phase(run, run, first)

    paired = ctx_count == heads
    if mp_count == 2:
        others = [lax.ppermute(run_states, "mp", [(0, 1), (1, 0)]) for run_states in (first[0], rest)]
        before, held = project(half[None], states, kv_weight)
        other_half = 1 - half
    else:
        others = [lax.all_gather(states, "mp", axis=0, tiled=True)]
        before = jnp.zeros((2 * slots, width), jnp.float32)
        other_half = jnp.zeros_like(half)
        held = kv_weight[:, :, : column_block(width)]
    if paired:
        sent, others[0] = lax.optimization_barrier((states, others[0]))
        query = lax.all_to_all(sent, "ctx", 0, 0, tiled=True).reshape(ctx_count * slots, HEAD)
    kv = project_more(other_half[None], others, kv_weight, held, before)

    valid = patch_bounds[:, 1:] > patch_bounds[:, :-1]
    if paired:
        bias = jnp.where(valid, 0.0, MASKED).astype(jnp.float32).reshape(1, ctx_count * slots)
        kv = lax.all_to_all(kv, "ctx", 0, 0, tiled=True).reshape(ctx_count * slots, 2 * HEAD)
        mixed = attend(bias, query, kv).reshape(ctx_count, slots, HEAD)
        mixed = lax.all_to_all(mixed, "ctx", 0, 0, tiled=True)
        mixed = mixed.transpose(1, 0, 2).reshape(slots, width)
    else:
        query, keys, values = (
            part.transpose(1, 0, 2).reshape(slots, width)
            for part in (states, kv[:, :, :HEAD], kv[:, :, HEAD:])
        )
        mixed = attend_gathered(place, valid.reshape(-1), query, keys, values)
    live = lax.dynamic_index_in_dim(valid, place, 0, keepdims=False)
    return jnp.where(live[:, None], mixed, jnp.zeros_like(mixed))


def solution(mesh):
    return jax.shard_map(
        shards,
        mesh=mesh,
        in_specs=(P("ctx", None, "mp"), P(None, None, "mp"), P()),
        out_specs=P("ctx", "mp"),
        check_vma=False,
    )
```

```python
import functools
import math

import jax
import jax.numpy as jnp
from jax import lax
from jax.experimental import pallas as pl
from jax.experimental.pallas import tpu as pltpu
from jax.sharding import PartitionSpec as P

D = 4096
HEADS = 32
WIN = 16
HEAD = D // HEADS
SCALE = 1.0 / math.sqrt(HEAD)
SCALE_2 = SCALE * math.log2(math.e)
MASKED = -1e30


def params(mebibytes):
    return pltpu.CompilerParams(vmem_limit_bytes=mebibytes * 1024 * 1024)


def dot_f32(left, right, right_dim=0):
    return lax.dot_general(
        left, right, (((1,), (right_dim,)), ((), ())), preferred_element_type=jnp.float32
    )


def ahead(row, steps):
    return pltpu.roll(row, row.shape[1] - steps, 1)


def outline_body(place_ref, bounds_ref, parts_ref, held_ref, pens, cuts, inside, pick, arrived):
    load = pltpu.make_async_copy(parts_ref.at[:, :, pl.ds(0, held_ref.shape[2])], held_ref, arrived)
    load.start()
    byte_rows = parts_ref.shape[1]
    slots, lanes = inside.shape
    rows = pens.shape[1]
    entries = bounds_ref.shape[1]
    place = place_ref[0]
    local = (bounds_ref[pl.ds(place, 1), :] - place * byte_rows).astype(jnp.float32)
    entry = lax.broadcasted_iota(jnp.int32, (slots, entries), 1)
    slot = lax.broadcasted_iota(jnp.int32, (slots, entries), 0)
    first = jnp.sum(jnp.where(entry == slot, local, 0.0), axis=1, keepdims=True)
    after = jnp.sum(jnp.where(entry == slot + 1, local, 0.0), axis=1, keepdims=True)
    byte = lax.broadcasted_iota(jnp.int32, (slots, lanes), 1).astype(jnp.float32)
    member = (byte >= first) & (byte < after)
    inside[...] = jnp.where(member, 1.0, 0.0)
    pick[...] = jnp.where(member & (byte == first), 1.0, 0.0)[:, :rows].astype(jnp.bfloat16)
    edges = jnp.where((byte == first) | (byte == after), 1.0, 0.0)
    cut = jnp.where(jnp.max(edges, axis=0, keepdims=True) > 0.0, -jnp.inf, 0.0)
    cut = ahead(jnp.broadcast_to(cut, (8, lanes)), 1)
    cuts[0] = cut
    at = lax.broadcasted_iota(jnp.int32, (rows, entries), 0).astype(jnp.float32)
    begins = jnp.max(jnp.where(at == local, 1.0, 0.0), axis=1, keepdims=True)
    pen = jnp.broadcast_to(jnp.where(begins > 0.0, -jnp.inf, 0.0), (rows, HEAD))
    pen = pltpu.roll(pen, rows - 1, 0)
    pens[0] = pen
    for level in range(1, 4):
        steps = 1 << (level - 1)
        cut = cut + ahead(cut, steps)
        cuts[level] = cut
        pen = pen + pltpu.roll(pen, rows - steps, 0)
        pens[level] = pen
    load.wait()


def outline(place, bounds, parts, slots):
    rows = parts.shape[1] + WIN
    lanes = -(-rows // 128) * 128
    in_vmem = pl.BlockSpec(memory_space=pltpu.VMEM)
    anywhere = pl.BlockSpec(memory_space=pl.ANY)
    found = pl.pallas_call(
        outline_body,
        in_specs=[pl.BlockSpec(memory_space=pltpu.SMEM), in_vmem, anywhere],
        out_specs=[anywhere] + [in_vmem] * 4,
        out_shape=[
            pltpu.VMEM((*parts.shape[:2], parts.shape[2] // 2), parts.dtype),
            pltpu.VMEM((4, rows, HEAD), jnp.float32),
            pltpu.VMEM((4, 8, lanes), jnp.float32),
            pltpu.VMEM((slots, lanes), jnp.float32),
            pltpu.VMEM((slots, rows), jnp.bfloat16),
        ],
        scratch_shapes=[pltpu.SemaphoreType.DMA],
        compiler_params=params(20),
        name="outline",
    )(place, bounds, parts)
    return [pltpu.with_memory_space_constraint(array, pltpu.VMEM) for array in found]


def patch_body(first_head, joins, main_ref, pens, cuts, inside, pick, edge_ref, *refs):
    if joins:
        lead_ref, rest_ref, out_ref, whole_ref, tops = refs
        held_back = rest_ref.shape[0]
        heads = out_ref.shape[0] - held_back
    else:
        parts_ref, lead_ref, rest_ref, next_ref, tops, arrived = refs
        run = pl.ds(next_ref.shape[2], next_ref.shape[2])
        load = pltpu.make_async_copy(parts_ref.at[:, :, run], next_ref, arrived)
        load.start()
        held_back = 0
        heads = lead_ref.shape[0] + rest_ref.shape[0]
    rows = pens.shape[1]
    lanes = inside.shape[1]

    def head_cols(head):
        return slice(head * HEAD, (head + 1) * HEAD)

    def edge_cols(head):
        return head_cols(first_head + head)

    for head in range(heads):
        cols = head_cols(head)
        top = jnp.concatenate([main_ref[0, :, cols], edge_ref[0, :, edge_cols(head)]], axis=0).astype(jnp.float32)
        for level in range(4):
            top = jnp.maximum(top, pltpu.roll(top, rows - (1 << level), 0) + pens[level])
        tops[:, head * HEAD : (head + 1) * HEAD] = top.astype(jnp.bfloat16)
    queries = dot_f32(pick[...], tops[...]).astype(jnp.bfloat16)
    spare = jnp.zeros((lanes - rows, HEAD), jnp.bfloat16)
    score_rows = []
    for head in range(heads):
        cols = head_cols(head)
        keys = jnp.concatenate([main_ref[1, :, cols], edge_ref[1, :, edge_cols(head)], spare], axis=0)
        scores = dot_f32(queries[:, head * HEAD : (head + 1) * HEAD], keys, 1) * inside[...]
        score_rows.append(jnp.sum(scores, axis=0, keepdims=True))
    scores = jnp.concatenate(score_rows + [jnp.zeros((8 - heads, lanes), jnp.float32)] * (heads < 8), axis=0)
    fore = back = scores
    for level in range(4):
        steps = 1 << level
        cut = cuts[level]
        fore = jnp.maximum(fore, ahead(fore, steps) + cut)
        back = jnp.maximum(back, pltpu.roll(back + cut, steps, 1))
    terms = jnp.exp((scores - jnp.maximum(fore, back)) * SCALE)
    fore = back = terms
    for level in range(4):
        steps = 1 << level
        keep = jnp.where(cuts[level] < 0.0, 0.0, 1.0)
        fore = fore + ahead(fore, steps) * keep
        back = back + pltpu.roll(back * keep, steps, 1)
    weights = terms / (fore + back - terms)
    for head in range(heads):
        cols = head_cols(head)
        values = jnp.concatenate([main_ref[2, :, cols], edge_ref[2, :, edge_cols(head)], spare], axis=0)
        spread = (inside[...] * weights[head : head + 1]).astype(jnp.bfloat16)
        states = dot_f32(spread, values).astype(jnp.bfloat16)
        if joins:
            out_ref[held_back + head] = states
        elif head < lead_ref.shape[0]:
            lead_ref[head] = states
        else:
            rest_ref[head - lead_ref.shape[0]] = states
    if joins:
        out_ref[:held_back] = rest_ref[...]
        whole_ref[: lead_ref.shape[0]] = lead_ref[...]
        whole_ref[lead_ref.shape[0] :] = out_ref[...]
    else:
        load.wait()


def patch_states(found, edge, first_head, heads, parts, earlier=()):
    slots, rows = found[-1].shape
    if earlier:
        counts = (earlier[1].shape[0] + heads, first_head + heads)
    else:
        lead = max(heads * 5 // 8, 1)
        counts = (lead, heads - lead)
    in_vmem = pl.BlockSpec(memory_space=pltpu.VMEM)
    anywhere = pl.BlockSpec(memory_space=pl.ANY)
    loads = not earlier
    out_shape = [jax.ShapeDtypeStruct((count, slots, HEAD), jnp.bfloat16) for count in counts]
    return pl.pallas_call(
        functools.partial(patch_body, first_head, bool(earlier)),
        in_specs=[in_vmem] * (len(found) + 1 + len(earlier)) + [anywhere] * loads,
        out_specs=[in_vmem, in_vmem] + [anywhere] * loads,
        out_shape=out_shape + [pltpu.VMEM(found[0].shape, found[0].dtype)] * loads,
        scratch_shapes=[pltpu.VMEM((rows, heads * HEAD), jnp.bfloat16)] + [pltpu.SemaphoreType.DMA] * loads,
        compiler_params=params(20),
        name="patch_states",
    )(*found, edge, *earlier, *([parts] if loads else []))


def column_block(width):
    return next(c for c in (512, 256, 128) if width % c == 0 and width > c)


def spread_states(states_refs, spread):
    slots = states_refs[0].shape[1]
    feature = lax.broadcasted_iota(jnp.int32, (HEAD, 2 * HEAD), 0)
    row = lax.broadcasted_iota(jnp.int32, (HEAD, 2 * HEAD), 1)
    for part in range(2):
        place = jnp.where(row == 2 * feature + part, 1.0, 0.0).astype(jnp.bfloat16)
        at = 0
        for states_ref in states_refs:
            for head in range(states_ref.shape[0]):
                spread[part * slots : (part + 1) * slots, at : at + 2 * HEAD] = dot_f32(
                    states_ref[head], place
                ).astype(jnp.bfloat16)
                at += 2 * HEAD


def project_body(half_ref, states_ref, weight_ref, sums_ref, held_ref, spread, blocks, arrived, held_arrived):
    count = states_ref.shape[0] * HEAD
    steps, _, _, block = blocks.shape
    half = half_ref[0]
    copies = [
        pltpu.make_async_copy(
            weight_ref.at[half_rows(half, count), :, pl.ds(step * block, block)],
            blocks.at[step],
            arrived.at[step],
        )
        for step in range(1, steps)
    ]
    near = count // 2
    starts = [
        pltpu.make_async_copy(
            weight_ref.at[pl.ds(pl.multiple_of(half * count + part * near, near), near), :, pl.ds(0, block)],
            blocks.at[0, pl.ds(part * near, near)],
            arrived.at[part * steps],
        )
        for part in range(2)
    ]
    hold = pltpu.make_async_copy(
        weight_ref.at[half_rows(1 - half, count), :, pl.ds(0, held_ref.shape[2])], held_ref, held_arrived
    )
    for copy in starts + copies:
        copy.start()
    hold.start()
    spread_states([states_ref], spread)
    weights = blocks.at[0].reshape(2 * count, block)
    starts[0].wait()
    product = dot_f32(spread[:, :count], weights[:count])
    starts[1].wait()
    sums_ref[:, :block] = product + dot_f32(spread[:, count:], weights[count:])
    for step in range(1, steps):
        copies[step - 1].wait()
        weights = blocks.at[step].reshape(2 * count, block)[...]
        sums_ref[:, step * block : (step + 1) * block] = dot_f32(spread[...], weights)
    hold.wait()


def half_rows(half, count):
    return pl.ds(pl.multiple_of(half * count, count), count)


def project(half, states, weight):
    heads, slots, _ = states.shape
    width = weight.shape[2]
    block = column_block(width)
    count = heads * HEAD
    in_vmem = pl.BlockSpec(memory_space=pltpu.VMEM)
    return pl.pallas_call(
        project_body,
        in_specs=[pl.BlockSpec(memory_space=pltpu.SMEM), in_vmem, pl.BlockSpec(memory_space=pl.ANY)],
        out_specs=[in_vmem, pl.BlockSpec(memory_space=pl.ANY)],
        out_shape=[
            jax.ShapeDtypeStruct((2 * slots, width), jnp.float32),
            pltpu.VMEM((count, 2, block), weight.dtype),
        ],
        scratch_shapes=[
            pltpu.VMEM((2 * slots, 2 * count), jnp.bfloat16),
            pltpu.VMEM((width // block, count, 2, block), jnp.bfloat16),
            pltpu.SemaphoreType.DMA((width // block + 1,)),
            pltpu.SemaphoreType.DMA,
        ],
        compiler_params=params(28),
        cost_estimate=pl.CostEstimate(
            flops=8 * slots * count * width, bytes_accessed=8 * count * width, transcendentals=0
        ),
        name="project",
    )(half, states, weight)


def project_more_body(runs, half_ref, *refs):
    states_refs, (weight_ref, held_ref, before_ref, out_ref, spread, blocks, arrived) = refs[:runs], refs[runs:]
    slots = out_ref.shape[1]
    count = spread.shape[1] // 2
    later_steps, _, _, block = blocks.shape
    copies = [
        pltpu.make_async_copy(
            weight_ref.at[half_rows(half_ref[0], count), :, pl.ds((step + 1) * block, block)],
            blocks.at[step],
            arrived.at[step],
        )
        for step in range(later_steps)
    ]
    for copy in copies:
        copy.start()
    spread_states(states_refs, spread)
    for step in range(later_steps + 1):
        if step:
            copies[step - 1].wait()
        weights = (blocks.at[step - 1] if step else held_ref).reshape(2 * count, block)[...]
        before = before_ref[:, step * block : (step + 1) * block]
        total = (before + dot_f32(spread[...], weights)).astype(jnp.bfloat16)
        for part in range(block // HEAD):
            head = step * (block // HEAD) + part
            cols = slice(part * HEAD, (part + 1) * HEAD)
            out_ref[head, :, :HEAD] = total[:slots, cols]
            out_ref[head, :, HEAD:] = total[slots:, cols]


def project_more(half, states, weight, held, before):
    slots = states[0].shape[1]
    width = weight.shape[2]
    block = held.shape[2]
    later_steps = width // block - 1
    count = sum(run_states.shape[0] for run_states in states) * HEAD
    in_vmem = pl.BlockSpec(memory_space=pltpu.VMEM)
    return pl.pallas_call(
        functools.partial(project_more_body, len(states)),
        in_specs=[pl.BlockSpec(memory_space=pltpu.SMEM)]
        + [in_vmem] * len(states)
        + [pl.BlockSpec(memory_space=pl.ANY), in_vmem, in_vmem],
        out_specs=in_vmem,
        out_shape=jax.ShapeDtypeStruct((width // HEAD, slots, 2 * HEAD), jnp.bfloat16),
        scratch_shapes=[
            pltpu.VMEM((2 * slots, 2 * count), jnp.bfloat16),
            pltpu.VMEM((later_steps, count, 2, block), weight.dtype),
            pltpu.SemaphoreType.DMA((later_steps,)),
        ],
        compiler_params=params(28),
        cost_estimate=pl.CostEstimate(
            flops=8 * slots * count * width, bytes_accessed=4 * count * width, transcendentals=0
        ),
        name="project_more",
    )(half, *states, weight, pltpu.with_memory_space_constraint(held, pltpu.VMEM), before)


def attend_body(block, bias_ref, query_ref, kv_ref, out_ref, values, scores, terms):
    slots = kv_ref.shape[0]
    count = slots // block
    values[:, :HEAD] = kv_ref[:, HEAD:]
    values[:, HEAD:] = jnp.ones((slots, HEAD), jnp.bfloat16)
    row = lax.broadcasted_iota(jnp.int32, (block, block), 0)
    col = lax.broadcasted_iota(jnp.int32, (block, block), 1)
    later = jnp.where(col <= row, 0.0, MASKED)
    top = [None] * count

    def tile(index):
        return slice(index * block, (index + 1) * block)

    def score(at, index):
        found = dot_f32(query_ref[tile(at)], kv_ref[tile(index), :HEAD], 1) * SCALE_2 + bias_ref[:, tile(index)]
        if index == at:
            found = found + later
        scores[at % 2, :, tile(index)] = found
        for lane in range(0, block, 128):
            part = found[:, lane : lane + 128]
            top[at] = part if top[at] is None else jnp.maximum(top[at], part)
        if index == at:
            top[at] = jnp.max(top[at], axis=1, keepdims=True)

    def term(at, index):
        found = jnp.exp2(scores[at % 2, :, tile(index)] - top[at])
        high = found.astype(jnp.bfloat16)
        terms[at % 2, 0, :, tile(index)] = high
        terms[at % 2, 1, :, tile(index)] = (found - high.astype(jnp.float32)).astype(jnp.bfloat16)

    for at in range(-2, count):
        total = None
        for index in range(at + 3):
            if at + 1 < count and 0 <= at + 1 and index <= at + 1:
                term(at + 1, index)
            if 0 <= at and index <= at:
                part = dot_f32(terms[at % 2, 0, :, tile(index)], values[tile(index)]) + dot_f32(
                    terms[at % 2, 1, :, tile(index)], values[tile(index)]
                )
                total = part if total is None else total + part
            if at + 2 < count:
                score(at + 2, index)
        if 0 <= at:
            mixed = query_ref[tile(at)].astype(jnp.float32) + total[:, :HEAD] / total[:, HEAD:]
            out_ref[tile(at)] = mixed.astype(jnp.bfloat16)


def attend(bias, query, kv):
    slots = kv.shape[0]
    block = next(b for b in (256, 128) if slots % b == 0)
    return pl.pallas_call(
        functools.partial(attend_body, block),
        out_shape=jax.ShapeDtypeStruct((slots, HEAD), jnp.bfloat16),
        scratch_shapes=[
            pltpu.VMEM((slots, 2 * HEAD), jnp.bfloat16),
            pltpu.VMEM((2, block, slots), jnp.float32),
            pltpu.VMEM((2, 2, block, slots), jnp.bfloat16),
        ],
        compiler_params=params(28),
        name="attend",
    )(bias, query, kv)


def attend_gathered(place, valid, queries, keys, values):
    slots, width = queries.shape
    heads = width // HEAD
    keys = lax.all_gather(keys, "ctx", axis=0, tiled=True)
    values = lax.all_gather(values, "ctx", axis=0, tiled=True)
    total = keys.shape[0]
    query_slot = place * slots + jnp.arange(slots, dtype=jnp.int32)
    visible = (jnp.arange(total, dtype=jnp.int32)[None, :] <= query_slot[:, None]) & valid[None, :]
    scores = jnp.einsum(
        "qhd,khd->hqk",
        queries.reshape(slots, heads, HEAD),
        keys.reshape(total, heads, HEAD),
        preferred_element_type=jnp.float32,
    )
    scores = jnp.where(visible[None], scores * SCALE, MASKED)
    terms = jnp.where(visible[None], jnp.exp(scores - jnp.max(scores, axis=2, keepdims=True)), 0.0)
    sums = jnp.sum(terms, axis=2)
    attended = jnp.einsum(
        "hqk,khd->hqd",
        terms,
        values.reshape(total, heads, HEAD).astype(jnp.float32),
        precision=lax.Precision.HIGHEST,
    )
    attended = attended / jnp.where(sums > 0, sums, 1.0)[:, :, None]
    attended = attended.transpose(1, 0, 2).reshape(slots, width)
    return (queries.astype(jnp.float32) + attended).astype(jnp.bfloat16)


def shards(byte_qkv, kv_weight, patch_bounds):
    width = byte_qkv.shape[2]
    heads = width // HEAD
    slots = patch_bounds.shape[1] - 1
    ctx_count, mp_count = lax.axis_size("ctx"), lax.axis_size("mp")
    place = lax.axis_index("ctx").astype(jnp.int32)
    half = lax.axis_index("mp").astype(jnp.int32)

    edge = lax.ppermute(byte_qkv[:WIN], "ctx", [(i + 1, i) for i in range(ctx_count - 1)])
    parts = byte_qkv.transpose(1, 0, 2)
    edge = edge.transpose(1, 0, 2)
    in_hbm = functools.partial(pltpu.with_memory_space_constraint, memory_space=pltpu.HBM)
    found = outline(place[None], in_hbm(patch_bounds), in_hbm(parts), slots)
    run = heads // 2
    lead, held_back, second = patch_states(found, edge, 0, run, in_hbm(parts))
    found[0] = pltpu.with_memory_space_constraint(second, pltpu.VMEM)
    rest, states = patch_states(found, edge, run, run, None, (lead, held_back))

    paired = ctx_count == heads
    if mp_count == 2:
        others = [lax.ppermute(run_states, "mp", [(0, 1), (1, 0)]) for run_states in (lead, rest)]
        before, held = project(half[None], states, kv_weight)
        other_half = 1 - half
    else:
        others = [lax.all_gather(states, "mp", axis=0, tiled=True)]
        before = jnp.zeros((2 * slots, width), jnp.float32)
        other_half = jnp.zeros_like(half)
        held = kv_weight[:, :, : column_block(width)]
    if paired:
        sent, others[0] = lax.optimization_barrier((states, others[0]))
        query = lax.all_to_all(sent, "ctx", 0, 0, tiled=True).reshape(ctx_count * slots, HEAD)
    kv = project_more(other_half[None], others, kv_weight, held, before)

    valid = patch_bounds[:, 1:] > patch_bounds[:, :-1]
    if paired:
        bias = jnp.where(valid, 0.0, MASKED).astype(jnp.float32).reshape(1, ctx_count * slots)
        kv = lax.all_to_all(kv, "ctx", 0, 0, tiled=True).reshape(ctx_count * slots, 2 * HEAD)
        mixed = attend(bias, query, kv).reshape(ctx_count, slots, HEAD)
        mixed = lax.all_to_all(mixed, "ctx", 0, 0, tiled=True)
        mixed = mixed.transpose(1, 0, 2).reshape(slots, width)
    else:
        query, keys, values = (
            part.transpose(1, 0, 2).reshape(slots, width)
            for part in (states, kv[:, :, :HEAD], kv[:, :, HEAD:])
        )
        mixed = attend_gathered(place, valid.reshape(-1), query, keys, values)
    live = lax.dynamic_index_in_dim(valid, place, 0, keepdims=False)
    return jnp.where(live[:, None], mixed, jnp.zeros_like(mixed))


def solution(mesh):
    return jax.shard_map(
        shards,
        mesh=mesh,
        in_specs=(P("ctx", None, "mp"), P(None, None, "mp"), P()),
        out_specs=P("ctx", "mp"),
        check_vma=False,
    )
```
